512 devices in a mesh: dp: 128 (over z, y, core), out: 4 (over x).
Axes of the slice: x: 4, y: 8, z: 8, core: 2. Of those that a mesh axis runs over, the one named last changes fastest.
Arguments:
- points: bfloat16 [196608, 440], P('dp'), may hold values from -6 to 6
- weights: float32 [256, 196608], P('out', 'dp'), may hold values from -0.6 to 0.6
- targets: float32 [256, 196608], P('out', 'dp'), may hold values from -6 to 6
- fitted: float32 [256, 196608], P('out', 'dp'), may hold values from -6 to 6
- preconditioner: float32 [2, 1024, 1024], P(None, 'dp'), may hold values from -2 to 3
- owners: int32 [2], replicated, may hold values from 0 to 127
- block_index: int32 [2, 1024], replicated, may hold values from 0 to 1535, as said below
Outputs:
- new_weights: float32 [256, 196608], P('out', 'dp')
- new_fitted: float32 [256, 196608], P('out', 'dp')
The draws below stay inside these ranges and needn't reach their ends.
Inputs may be any that keep to these rules, and one draw needn't show every extreme that they name: `block_index`: within one step the 1024 point numbers are distinct.
All inputs are finite; a program needn't handle non-finite values.
Results may differ from the reference program's by a relative error of at most 0.0003.
Values may be sent and summed in bfloat16 or wider, within the bound.
No kernel may reach another device: no remote copies, remote signals or barrier semaphores. Data moves between devices by JAX's collectives and lax.ppermute only.
A program may use at most 64 MiB of HBM per device.

```python
import jax
import jax.numpy as jnp
from jax import lax

F = 440
OUT = 256
P_DEV = 1536
B = 1024
STEPS = 2
NPTS = 196608
N_DP = 128


def draw_points(key, part):
    key = jax.random.fold_in(key, 3)
    key_dir, key_coef, key_noise = jax.random.split(key, 3)
    directions = jax.random.normal(key_dir, (4, F), jnp.float32)
    coef = jax.random.normal(key_coef, (NPTS, 4), jnp.float32)
    noise = jax.random.normal(key_noise, (NPTS, F), jnp.float32)
    strength = 0.5
    spread = 0.6
    shared = coef[:, 0:1] * directions[0][None, :]
    shared = shared + coef[:, 1:2] * directions[1][None, :]
    shared = shared + coef[:, 2:3] * directions[2][None, :]
    shared = shared + coef[:, 3:4] * directions[3][None, :]
    return jnp.clip(strength * shared + spread * noise, -6.0, 6.0).astype(jnp.bfloat16)


def draw_preconditioner(key, part):
    key = jax.random.fold_in(key, 5)
    first, second = jax.random.split(key)
    diag = jax.random.uniform(first, (STEPS, B), jnp.float32, 0.5, 1.5)
    off = jax.random.normal(second, (STEPS, B, B), jnp.float32) * (0.5 / jnp.sqrt(B * 1.0))
    return off + jnp.eye(B, dtype=jnp.float32)[None] * diag[:, :, None]


def pick_rows(key):
    first, second = jax.random.split(key)
    inner = 1 + jax.random.permutation(first, P_DEV - 2)[:B - 2]
    ends = jnp.array([0, P_DEV - 1], dtype=jnp.int32)
    chosen = jnp.concatenate([ends, inner.astype(jnp.int32)])
    return jax.random.permutation(second, chosen)


def draw_block_index(key, part):
    key = jax.random.fold_in(key, 7)
    keys = jax.random.split(key, STEPS)
    return jax.vmap(pick_rows)(keys).astype(jnp.int32)


def block_scale(rng, dims, cuts, least, high):
    loudness, own = 1.0, jax.random.fold_in(rng, 6)
    for axis_at, shards_of in cuts:
        draws = jnp.exp(jax.random.uniform(jax.random.fold_in(own, axis_at), (shards_of,), jnp.float32, least / len(cuts), high / len(cuts)))
        loudness = loudness * jnp.repeat(draws, dims[axis_at] // shards_of).reshape([-1 if axis == axis_at else 1 for axis in range(len(dims))])
    return loudness


def normal_values(stream_key, extent, scale, limit, pieces=(), kind=jnp.bfloat16):
    result = jax.random.normal(stream_key, extent, jnp.float32) * scale
    if len(pieces) > 0:
        result = block_scale(stream_key, extent, pieces, -0.22, 0.18) * result
    return jnp.clip(result, min=-limit, max=limit).astype(kind)


def setup_inputs(seed: int = 0) -> dict:
    arg_keys = jax.random.split(jax.random.key(seed), 8)
    points = draw_points(jax.random.fold_in(arg_keys[7], 71), 0)
    weights = normal_values(arg_keys[1], (OUT, NPTS), 0.1, 0.6, ((0, 4), (1, 128)), jnp.float32)
    targets = normal_values(arg_keys[2], (OUT, NPTS), 1.0, 6.0, ((0, 4), (1, 128)), jnp.float32)
    fitted = normal_values(arg_keys[3], (OUT, NPTS), 1.0, 6.0, ((0, 4), (1, 128)), jnp.float32)
    preconditioner = draw_preconditioner(jax.random.fold_in(arg_keys[7], 71), 0)
    owners = jax.random.randint(arg_keys[5], (STEPS,), 0, N_DP).astype(jnp.int32)
    block_index = draw_block_index(jax.random.fold_in(arg_keys[7], 71), 0)
    return {"points": points, "weights": weights, "targets": targets, "fitted": fitted, "preconditioner": preconditioner, "owners": owners, "block_index": block_index}


LAMBDA = 0.5


def kernel_block(shard, block, block_norm, gamma):
    cross = jnp.dot(shard, block.T, preferred_element_type=jnp.float32)
    wide = shard.astype(jnp.float32)
    shard_norm = jnp.sum(wide * wide, axis=1)
    return jnp.exp(-gamma * (shard_norm[:, None] + block_norm[None, :] - 2.0 * cross))


def reference(points, weights, targets, fitted, preconditioner, owners, block_index):
    gamma = 2.0 / F
    shards = points.reshape(N_DP, P_DEV, F)
    for step in range(STEPS):
        rows = (owners[step] * P_DEV + block_index[step]).astype(jnp.int32)
        block = points[rows]
        wide = block.astype(jnp.float32)
        block_norm = jnp.sum(wide * wide, axis=1)
        weight_shards = jnp.transpose(weights.reshape(OUT, N_DP, P_DEV), (1, 0, 2))

        def accumulate(carry, pair):
            kern = kernel_block(pair[0], block, block_norm, gamma)
            return carry + jnp.dot(pair[1], kern, precision=lax.Precision.HIGHEST), None

        total, _ = lax.scan(accumulate, jnp.zeros((OUT, B), jnp.float32), (shards, weight_shards))
        grad = total + LAMBDA * weights[:, rows] - targets[:, rows]
        delta = jnp.dot(grad, preconditioner[step].T, precision=lax.Precision.HIGHEST)
        fit_shards = jnp.transpose(fitted.reshape(OUT, N_DP, P_DEV), (1, 0, 2))

        def refit(pair):
            kern = kernel_block(pair[0], block, block_norm, gamma)
            return pair[1] - jnp.dot(delta, kern.T, precision=lax.Precision.HIGHEST)

        refitted = lax.map(refit, (shards, fit_shards))
        fitted = jnp.transpose(refitted, (1, 0, 2)).reshape(OUT, NPTS)
        weights = weights.at[:, rows].add(-delta)
    return weights, fitted
```

```python
import jax
import jax.numpy as jnp
from jax import lax
from jax.sharding import Mesh, PartitionSpec as P

LAMBDA = 0.5
GRID = (8, 8, 2)
ZY = ("z", "y")
DP = ("z", "y", "c")
FEATURE_ROWS = 512
HIGH = lax.Precision.HIGH


def exchange(value):
    return lax.ppermute(value, "c", [(0, 1), (1, 0)])


def by_core(core, mine, other, axis):
    first = jnp.where(core == 0, mine, other)
    second = jnp.where(core == 0, other, mine)
    return jnp.concatenate([first, second], axis=axis)


def all_to_all(value, axes):
    return lax.all_to_all(value, axes, 0, 0, tiled=True)


def three_parts(value):
    high = lax.reduce_precision(value, 8, 7)
    rest = value - high
    middle = lax.reduce_precision(rest, 8, 7)
    low = rest - middle
    return jnp.concatenate([high, middle, low], axis=0).astype(jnp.bfloat16)


def sum_parts(value):
    high, middle, low = jnp.split(value, 3, axis=0)
    return high + (middle + low)


def gauss(gamma, left_norm, right_norm, cross):
    return jnp.exp(-gamma * (left_norm[:, None] + right_norm[None, :] - 2.0 * cross))


def broadcast_blocks(points, index, owners, zy, core, column):
    groups, lines, cores = GRID[0] * GRID[1], lax.axis_size("x"), GRID[2]
    steps, block = index.shape
    count, features = points.shape
    quarter = block // lines
    half = quarter // cores
    mine = lax.dynamic_slice(index, (0, column * quarter), (steps, quarter))
    ident = lax.broadcasted_iota(jnp.int32, (count, steps * quarter), 0)
    pick = (ident == mine.reshape(1, -1)).astype(jnp.bfloat16)
    candidate = lax.dot_general(
        points, pick, (((0,), (0,)), ((), ())), preferred_element_type=jnp.float32
    ).astype(jnp.bfloat16)
    candidate = jnp.pad(candidate, ((0, FEATURE_ROWS - features), (0, 0)))
    candidate = candidate.reshape(FEATURE_ROWS, steps, cores, half)
    halves = [
        jnp.stack([candidate[:, s, k] for s in range(steps)]) for k in range(cores)
    ]
    keep = jnp.where(core == 0, halves[0], halves[1])
    send = jnp.where(core == 0, halves[1], halves[0])
    got = exchange(send)
    owner_core = owners % cores
    owner_zy = owners // cores
    own = jnp.stack(
        [jnp.where(owner_core[s] == core, keep[s], got[s]) for s in range(steps)]
    )
    rows = FEATURE_ROWS // groups
    parcels = own.reshape(steps, groups, rows, half).transpose(1, 0, 2, 3)
    parcels = all_to_all(parcels.reshape(groups, steps * rows, half), ZY)
    piece = jnp.concatenate(
        [
            lax.dynamic_slice(
                parcels, (owner_zy[s], s * rows, 0), (1, rows, half)
            )
            for s in range(steps)
        ],
        axis=1,
    )
    gathered = all_to_all(jnp.broadcast_to(piece, (groups, steps * rows, half)), ZY)
    gathered = gathered.reshape(groups, steps, rows, half).transpose(1, 0, 2, 3)
    gathered = gathered.reshape(1, steps * FEATURE_ROWS, half)
    gathered = all_to_all(
        jnp.broadcast_to(gathered, (lines, steps * FEATURE_ROWS, half)), "x"
    )
    other = exchange(gathered)
    first = jnp.where(core == 0, gathered, other)
    second = jnp.where(core == 0, other, gathered)
    both = jnp.stack([first, second])
    both = both.reshape(cores, lines, steps, FEATURE_ROWS, half)[:, :, :, :features]
    return both.transpose(2, 3, 1, 0, 4).reshape(steps, features, block)


def local(points, weights, targets, fitted, preconditioner, owners, block_index):
    gamma = 2.0 / points.shape[1]
    steps, block = block_index.shape
    count = points.shape[0]
    outs = weights.shape[0]
    cores = GRID[2]
    groups = GRID[0] * GRID[1]
    rows = preconditioner.shape[1]
    part = groups * rows
    core = lax.axis_index("c")
    zy = lax.axis_index(ZY)
    rank = zy * cores + core
    column = lax.axis_index("x")

    gathered = lax.all_gather(preconditioner, ZY, axis=0)

    index = block_index.reshape(steps, groups, cores, rows).transpose(0, 2, 1, 3)
    index = index.reshape(steps, block)

    blocks = broadcast_blocks(points, index, owners, zy, core, column)
    wide_blocks = blocks.astype(jnp.float32)
    norms = jnp.sum(wide_blocks * wide_blocks, axis=1)

    def columns(value):
        lead = value.shape[1:-1]
        value = value.reshape(steps, *lead, cores, part)
        value = jnp.moveaxis(value, 0, -2)
        return value.reshape(*lead, cores * steps * part)

    all_blocks = columns(blocks)
    all_norms = columns(norms)
    wide_points = points.astype(jnp.float32)
    point_norm = jnp.sum(wide_points * wide_points, axis=1)
    cross = jnp.dot(points, all_blocks, preferred_element_type=jnp.float32)
    kern = gauss(gamma, point_norm, all_norms, cross)

    owned_index = jnp.where((owners == rank)[:, None], index, -1)
    ident = lax.broadcasted_iota(jnp.int32, (count, steps * block), 0)
    pick = (ident == columns(owned_index)[None, :]).astype(jnp.bfloat16)

    own = sum_parts(
        jnp.dot(
            three_parts(LAMBDA * weights - targets),
            pick,
            preferred_element_type=jnp.float32,
        )
    )
    grad = jnp.dot(weights, kern, precision=HIGH) + own

    lanes = 128
    grad = all_to_all(grad.reshape(outs, -1, lanes), ZY)
    grad = jnp.sum(grad.reshape(groups, -1, lanes), axis=0)
    grad = (grad + exchange(grad)).reshape(cores, steps, groups, rows)

    cross = lax.dot_general(
        blocks[0],
        blocks[1],
        (((0,), (0,)), ((), ())),
        preferred_element_type=jnp.float32,
    )
    between = gauss(gamma, norms[0], norms[1], cross)
    same = (owners[0] == owners[1]) & (index[0][:, None] == index[1][None, :])
    between = between + jnp.where(same, LAMBDA, 0.0)

    def outer_order(value):
        return value.reshape(cores, groups, rows).transpose(1, 0, 2).reshape(block)

    def precondition(step, value):
        value = outer_order(value)
        return jnp.sum(gathered[:, step] * value[None, None, :], axis=-1)

    first = precondition(0, grad[:, 0])
    whole = by_core(core, first, exchange(first), 0).reshape(block)
    correction = jnp.sum(whole[:, None] * between, axis=0)
    second = precondition(1, grad[:, 1].reshape(block) - correction)

    delta = jnp.concatenate([first.reshape(1, part), second.reshape(1, part)], axis=1)
    delta = delta.reshape(1, -1, lanes)
    delta = all_to_all(jnp.broadcast_to(delta, (groups, *delta.shape[1:])), ZY)
    delta = delta.reshape(outs, steps * part)
    delta = by_core(core, delta, exchange(delta), 1)

    fitted = fitted - lax.dot_general(
        delta, kern, (((1,), (1,)), ((), ())), precision=HIGH
    )
    change = lax.dot_general(
        three_parts(delta),
        pick,
        (((1,), (1,)), ((), ())),
        preferred_element_type=jnp.float32,
    )
    weights = weights - sum_parts(change)
    return (weights, fitted)


def solution(mesh):
    lines = mesh.shape["out"]
    grid = Mesh(mesh.devices.reshape(*GRID, lines), (*DP, "x"))
    return jax.shard_map(
        local,
        mesh=grid,
        in_specs=(
            P(DP, None),
            P("x", DP),
            P("x", DP),
            P("x", DP),
            P(None, DP, None),
            P(),
            P(),
        ),
        out_specs=(P("x", DP), P("x", DP)),
        check_vma=False,
    )
```

```python
import functools

import jax
import jax.numpy as jnp
from jax import lax
from jax.experimental import pallas as pl
from jax.experimental.pallas import tpu as pltpu
from jax.sharding import Mesh, PartitionSpec as P

LAMBDA = 0.5
GRID = (8, 8, 2)
ZY = ("z", "y")
DP = ("z", "y", "c")
FEATURE_ROWS = 512
LANES = 128
CHUNK = 256
VMEM_BYTES = 48 * 1024 * 1024
BF16 = jnp.bfloat16
F32 = jnp.float32
TRANSPOSED = (((1,), (1,)), ((), ()))
FIRST_DIMS = (((0,), (0,)), ((), ()))

CORE, LINE, OWNS, SAME_OWNER = 0, 1, 2, 4


def params():
    return pltpu.CompilerParams(vmem_limit_bytes=VMEM_BYTES)


def exchange(value):
    return lax.ppermute(value, "c", [(0, 1), (1, 0)])


def all_to_all(value, axes):
    return lax.all_to_all(value, axes, 0, 0, tiled=True)


def two_parts(value):
    high = value.astype(BF16)
    return high, (value - high.astype(F32)).astype(BF16)


def three_parts(value):
    high = value.astype(BF16)
    rest = value - high.astype(F32)
    middle = rest.astype(BF16)
    return high, middle, (rest - middle.astype(F32)).astype(BF16)


def dot(left, right, dims=(((1,), (0,)), ((), ()))):
    return lax.dot_general(left, right, dims, preferred_element_type=F32)


def one_hot(count, numbers):
    rows = lax.broadcasted_iota(jnp.int32, (count, numbers.shape[1]), 0)
    return jnp.where(rows == numbers, 1.0, 0.0).astype(BF16)


def index_tile(index_ref, step, line, kind):
    return index_ref[step, pl.ds(2 * line + kind, 1), :]


def pick_kernel(info, points_ref, index_ref, keep_ref, send_ref):
    count, features = points_ref.shape
    steps = index_ref.shape[0]
    core, line = info[CORE], info[LINE]
    numbers = [
        index_tile(index_ref, step, line, kind)
        for kind in (core, 1 - core)
        for step in range(steps)
    ]
    picked = dot(points_ref[...], one_hot(count, jnp.concatenate(numbers, axis=1)), FIRST_DIMS)
    empty = jnp.zeros((FEATURE_ROWS - features, picked.shape[1]), F32)
    picked = jnp.concatenate([picked, empty], axis=0).astype(BF16)
    for place, ref in enumerate((keep_ref, send_ref)):
        for step in range(steps):
            at = (place * steps + step) * LANES
            ref[step] = picked[:, at : at + LANES]


def pick_blocks(info, points, index):
    steps = index.shape[0]
    shape = jax.ShapeDtypeStruct((steps, FEATURE_ROWS, LANES), BF16)
    return pl.pallas_call(
        pick_kernel,
        grid_spec=pltpu.PrefetchScalarGridSpec(
            num_scalar_prefetch=1,
            grid=(),
            in_specs=[pl.BlockSpec(memory_space=pltpu.VMEM)] * 2,
            out_specs=[pl.BlockSpec(memory_space=pltpu.VMEM)] * 2,
        ),
        out_shape=[shape, shape],
        compiler_params=params(),
        name="pick_blocks",
    )(info, points, index)


def kernel_kernel(
    foreign,
    info,
    points_ref,
    weights_ref,
    targets_ref,
    index_ref,
    blocks_ref,
    grad_ref,
    high_ref,
    low_ref,
    parts,
    norms,
):
    count, features = points_ref.shape
    outs = weights_ref.shape[0]
    gamma = 2.0 / features
    step, pair = pl.program_id(0), pl.program_id(1)

    @pl.when((step == 0) & (pair == 0))
    def _():
        high, low = two_parts(weights_ref[...])
        parts[:outs, :] = high
        parts[outs:, :] = low
        for at in range(0, count, CHUNK):
            wide = points_ref[at : at + CHUNK, :].astype(F32)
            norms[at : at + CHUNK, :] = gamma * jnp.sum(wide * wide, axis=1, keepdims=True)

    block = jnp.concatenate([blocks_ref[0], blocks_ref[1]], axis=1)
    wide = block.astype(F32)
    block_norm = gamma * jnp.sum(wide * wide, axis=0, keepdims=True)
    grad = jnp.zeros((outs, 2 * LANES), F32)
    for at in range(0, count, CHUNK):
        rows = slice(at, at + CHUNK)
        cross = dot(points_ref[rows, :], block[:features, :])
        kern = jnp.exp((2.0 * gamma) * cross - (norms[rows, :] + block_norm))
        high, low = two_parts(kern)
        high_ref[0, 0, rows, :] = high
        low_ref[0, 0, rows, :] = low
        both = dot(parts[:, rows], high)
        grad = grad + (both[:outs] + both[outs:] + dot(parts[:outs, rows], low))
    grad_ref[0, 0] = grad

    @pl.when(info[OWNS + step] == 1)
    def _():
        kind = info[CORE] ^ foreign
        numbers = [index_tile(index_ref, step, 2 * pair + k, kind) for k in range(2)]
        pick = one_hot(count, jnp.concatenate(numbers, axis=1))
        own = LAMBDA * weights_ref[...] - targets_ref[...]
        terms = [dot(part, pick) for part in three_parts(own)]
        grad_ref[0, 0] += terms[0] + (terms[1] + terms[2])


def kernel_and_gradient(foreign, info, points, weights, targets, index, blocks):
    count = points.shape[0]
    outs = weights.shape[0]
    steps = index.shape[0]
    pairs = blocks.shape[0] // 2
    whole = pl.BlockSpec(memory_space=pltpu.VMEM)
    kern_shape = jax.ShapeDtypeStruct((steps, pairs, count, 2 * LANES), BF16)
    kern_spec = pl.BlockSpec((1, 1, count, 2 * LANES), lambda s, p, info: (s, p, 0, 0))
    return pl.pallas_call(
        functools.partial(kernel_kernel, foreign),
        grid_spec=pltpu.PrefetchScalarGridSpec(
            num_scalar_prefetch=1,
            grid=(steps, pairs),
            in_specs=[whole] * 4
            + [pl.BlockSpec((2, FEATURE_ROWS, LANES), lambda s, p, info: (p, s, 0))],
            out_specs=[
                pl.BlockSpec((1, 1, outs, 2 * LANES), lambda s, p, info: (s, p, 0, 0)),
                kern_spec,
                kern_spec,
            ],
            scratch_shapes=[
                pltpu.VMEM((2 * outs, count), BF16),
                pltpu.VMEM((count, 1), F32),
            ],
        ),
        out_shape=[
            jax.ShapeDtypeStruct((steps, pairs, outs, 2 * LANES), F32),
            kern_shape,
            kern_shape,
        ],
        compiler_params=params(),
        name="kernel_and_gradient",
    )(info, points, weights, targets, index, blocks)


def between_kernel(features, info, index_ref, own_ref, other_ref, out_ref):
    lines = own_ref.shape[0]
    gamma = 2.0 / features
    core = info[CORE]

    def tile(step, line, kind):
        at = step * FEATURE_ROWS
        rows = slice(at, at + FEATURE_ROWS)
        return jnp.where(core == kind, own_ref[line, rows, :], other_ref[line, rows, :])

    places = [(line, kind) for line in range(lines) for kind in range(2)]
    second = jnp.concatenate([tile(1, *place) for place in places], axis=1)
    wide = second.astype(F32)
    second_norm = gamma * jnp.sum(wide * wide, axis=0, keepdims=True)
    second_index = jnp.concatenate(
        [index_ref[1, n : n + 1, :] for n in range(len(places))], axis=1
    )
    extra = jnp.where(info[SAME_OWNER] == 1, LAMBDA, 0.0)
    for n, place in enumerate(places):
        first = tile(0, *place)
        wide = first.astype(F32)
        square = jnp.sum(wide * wide, axis=0, keepdims=True)
        first_norm = gamma * jnp.transpose(jnp.broadcast_to(square, (LANES, LANES)))[:, :1]
        first_index = jnp.transpose(
            jnp.broadcast_to(index_ref[0, n : n + 1, :].astype(F32), (LANES, LANES))
        )[:, :1].astype(jnp.int32)
        cross = dot(first, second, FIRST_DIMS)
        kern = jnp.exp((2.0 * gamma) * cross - (first_norm + second_norm))
        out_ref[n * LANES : (n + 1) * LANES, :] = kern + jnp.where(
            first_index == second_index, extra, 0.0
        )


def between_blocks(features, info, index, own, other):
    block = index.shape[1] * LANES
    whole = pl.BlockSpec(memory_space=pltpu.VMEM)
    return pl.pallas_call(
        functools.partial(between_kernel, features),
        grid_spec=pltpu.PrefetchScalarGridSpec(
            num_scalar_prefetch=1, grid=(), in_specs=[whole] * 3, out_specs=whole
        ),
        out_shape=jax.ShapeDtypeStruct((block, block), F32),
        compiler_params=params(),
        cost_estimate=pl.CostEstimate(
            flops=2 * block * block * FEATURE_ROWS,
            bytes_accessed=4 * block * block,
            transcendentals=block * block,
        ),
        name="between_blocks",
    )(info, index, own, other)


def chain_kernel(info, mine_ref, theirs_ref, given_ref, between_ref, out_ref, grads, sums):
    step, part = pl.program_id(0), pl.program_id(1)
    parts = pl.num_programs(1)
    tiles = out_ref.shape[1]
    lines = tiles // 2
    core = info[CORE]

    @pl.when((step == 0) & (part == 0))
    def _():
        half = 2 * lines
        own = mine_ref[:half, :] + theirs_ref[half:, :]
        other = mine_ref[half:, :] + theirs_ref[:half, :]
        for s in range(2):
            for line in range(lines):
                at = slice(s * lines + line, s * lines + line + 1)
                for kind in range(2):
                    lanes = slice((2 * line + kind) * LANES, (2 * line + kind + 1) * LANES)
                    grads[s : s + 1, lanes] = jnp.where(core == kind, own[at, :], other[at, :])
        sums[...] = jnp.zeros_like(sums)

    @pl.when((step == 1) & (part == 0))
    def _():
        total = jnp.sum(sums[...], axis=0, keepdims=True)
        grads[1:2, :] = grads[1:2, :] - total

    grad = grads[pl.ds(step, 1), :]
    given = given_ref[...]
    given = given.reshape(-1, given.shape[-1])
    delta = jnp.sum(given * grad, axis=1, keepdims=True)

    @pl.when(step == 0)
    def _():
        product = delta * between_ref[...]
        sums[...] += jnp.sum(product.reshape(-1, *sums.shape), axis=0)

    diagonal = lax.broadcasted_iota(jnp.int32, (LANES, LANES), 0) == lax.broadcasted_iota(
        jnp.int32, (LANES, LANES), 1
    )
    rows = given.shape[0]
    for n in range(rows // LANES):
        column = delta[n * LANES : (n + 1) * LANES, :]
        row = jnp.sum(jnp.where(diagonal, column, 0.0), axis=0, keepdims=True)
        out_ref[pl.ds(step, 1), pl.ds(part * (rows // LANES) + n, 1), :] = row[None]


def run_chain(info, mine, theirs, given, between):
    devices, steps, rows, block = given.shape
    parts = 4
    share = devices // parts
    whole = pl.BlockSpec(memory_space=pltpu.VMEM)
    return pl.pallas_call(
        chain_kernel,
        grid_spec=pltpu.PrefetchScalarGridSpec(
            num_scalar_prefetch=1,
            grid=(steps, parts),
            in_specs=[
                whole,
                whole,
                pl.BlockSpec((share, 1, rows, block), lambda s, p, info: (p, s, 0, 0)),
                pl.BlockSpec(
                    (share * rows, block),
                    lambda s, p, info: (jnp.where(s == 0, p, parts - 1), 0),
                ),
            ],
            out_specs=whole,
            scratch_shapes=[pltpu.VMEM((steps, block), F32), pltpu.VMEM((8, block), F32)],
        ),
        out_shape=jax.ShapeDtypeStruct((steps, block // LANES, LANES), F32),
        compiler_params=params(),
        name="run_chain",
    )(info, mine, theirs, given, between)


def update_kernel(
    foreign,
    info,
    delta_ref,
    index_ref,
    weights_ref,
    fitted_ref,
    own_high,
    own_low,
    other_high,
    other_low,
    new_weights_ref,
    new_fitted_ref,
):
    pair = pl.program_id(0)
    core = info[CORE]
    step = core ^ foreign
    outs, count = weights_ref.shape

    @pl.when(pair == 0)
    def _():
        new_weights_ref[...] = weights_ref[...]
        new_fitted_ref[...] = fitted_ref[...]

    def tile(kind):
        tiles = [
            delta_ref[:, pl.ds(2 * (2 * pair + k) + kind, 1), :].reshape(outs, LANES)
            for k in range(2)
        ]
        return jnp.concatenate(tiles, axis=1)

    for high_ref, low_ref, kind in (
        (own_high, own_low, core),
        (other_high, other_low, 1 - core),
    ):
        delta = tile(kind)
        high, low = two_parts(delta)
        both = jnp.concatenate([high, low], axis=0)
        for at in range(0, count, CHUNK):
            rows = slice(at, at + CHUNK)
            change = dot(both, high_ref[0, 0, rows, :], TRANSPOSED)
            small = dot(high, low_ref[0, 0, rows, :], TRANSPOSED)
            new_fitted_ref[:, rows] -= change[:outs] + (change[outs:] + small)

        @pl.when(info[OWNS + step] == 1)
        def _():
            numbers = [index_tile(index_ref, step, 2 * pair + k, kind) for k in range(2)]
            pick = one_hot(count, jnp.concatenate(numbers, axis=1))
            terms = [dot(part, pick, TRANSPOSED) for part in three_parts(delta)]
            new_weights_ref[...] -= terms[0] + (terms[1] + terms[2])


def update(foreign, info, delta, index, weights, fitted, own, other):
    outs, count = weights.shape
    pairs = own[0].shape[1]
    whole = pl.BlockSpec(memory_space=pltpu.VMEM)
    kern_spec = pl.BlockSpec(
        (1, 1, count, 2 * LANES), lambda p, info: (info[CORE] ^ foreign, p, 0, 0)
    )
    shape = jax.ShapeDtypeStruct((outs, count), F32)
    return pl.pallas_call(
        functools.partial(update_kernel, foreign),
        grid_spec=pltpu.PrefetchScalarGridSpec(
            num_scalar_prefetch=1,
            grid=(pairs,),
            in_specs=[whole] * 4 + [kern_spec] * 4,
            out_specs=[whole, whole],
        ),
        out_shape=[shape, shape],
        compiler_params=params(),
        name="update",
    )(info, delta, index, weights, fitted, *own, *other)


def local(points, weights, targets, fitted, preconditioner, owners, block_index):
    steps, block = block_index.shape
    features = points.shape[1]
    outs = weights.shape[0]
    cores = GRID[2]
    groups = GRID[0] * GRID[1]
    lines = lax.axis_size("x")
    core = lax.axis_index("c")
    zy = lax.axis_index(ZY)
    rank = zy * cores + core

    given = lax.all_gather(preconditioner, DP, axis=0)
    owns = (owners == rank).astype(jnp.int32)
    same = (owners[0] == owners[1]).astype(jnp.int32)
    info = jnp.stack([core, lax.axis_index("x"), owns[0], owns[1], same])
    index = block_index.reshape(steps, block // LANES, LANES)

    keep, send = pick_blocks(info, points, index)
    got = exchange(send)
    owner_core = (owners % cores).reshape(steps, 1, 1)
    parcels = jnp.where(owner_core == core, keep, got)
    parcels = all_to_all(parcels.reshape(groups, -1, LANES), ZY)
    holder = owners[zy // (groups // steps)] // cores
    piece = lax.dynamic_index_in_dim(parcels, holder, 0)
    blocks = all_to_all(jnp.broadcast_to(piece, parcels.shape), ZY)
    blocks = blocks.reshape(1, steps * FEATURE_ROWS, LANES)
    own = all_to_all(jnp.broadcast_to(blocks, (lines, *blocks.shape[1:])), "x")
    other = exchange(own)

    grad_own, *kern_own = kernel_and_gradient(0, info, points, weights, targets, index, own)
    grad_other, *kern_other = kernel_and_gradient(
        1, info, points, weights, targets, index, other
    )
    grad = jnp.stack([grad_own, grad_other]).transpose(3, 0, 1, 2, 4)
    grad = all_to_all(grad.reshape(outs, -1, LANES), ZY)
    grad = jnp.sum(grad, axis=0)
    theirs = exchange(grad)
    between = between_blocks(features, info, index, own, other)
    delta = run_chain(info, grad, theirs, given, between)

    mine = lax.dynamic_index_in_dim(delta, core, 0)
    mine = all_to_all(jnp.broadcast_to(mine, (groups, *mine.shape[1:])), ZY)
    theirs = exchange(mine)
    weights, fitted = update(0, info, mine, index, weights, fitted, kern_own, kern_other)
    weights, fitted = update(1, info, theirs, index, weights, fitted, kern_own, kern_other)
    return (weights, fitted)


def solution(mesh):
    grid = Mesh(mesh.devices.reshape(*GRID, mesh.shape["out"]), (*DP, "x"))
    return jax.shard_map(
        local,
        mesh=grid,
        in_specs=(
            P(DP, None),
            P("x", DP),
            P("x", DP),
            P("x", DP),
            P(None, DP, None),
            P(),
            P(),
        ),
        out_specs=(P("x", DP), P("x", DP)),
        check_vma=False,
    )
```

```python
import functools

import jax
import jax.numpy as jnp
from jax import lax
from jax.experimental import pallas as pl
from jax.experimental.pallas import tpu as pltpu
from jax.sharding import Mesh, PartitionSpec as P

LAMBDA = 0.5
GRID = (8, 8, 2)
ZY = ("z", "y")
DP = ("z", "y", "c")
FEATURE_ROWS = 512
LANES = 128
CHUNK = 256
UNIT = 768
VMEM_BYTES = 16 * 1024 * 1024
BF16 = jnp.bfloat16
F32 = jnp.float32
TRANSPOSED = (((1,), (1,)), ((), ()))
FIRST_DIMS = (((0,), (0,)), ((), ()))
WHOLE = pl.BlockSpec(memory_space=pltpu.VMEM)


def call(kernel, name, shapes, owners, *args, scratch=(), aliases=None, cost=None):
    return pl.pallas_call(
        kernel,
        grid_spec=pltpu.PrefetchScalarGridSpec(
            num_scalar_prefetch=1,
            grid=(),
            in_specs=[WHOLE] * len(args),
            out_specs=[WHOLE] * len(shapes),
            scratch_shapes=list(scratch),
        ),
        out_shape=[jax.ShapeDtypeStruct(*shape) for shape in shapes],
        input_output_aliases=aliases or {},
        compiler_params=pltpu.CompilerParams(vmem_limit_bytes=VMEM_BYTES),
        cost_estimate=cost,
        name=name,
    )(owners, *args)


def my_rank():
    return (lax.axis_index("z") * GRID[1] + lax.axis_index("y")) * GRID[2] + lax.axis_index("c")


def exchange(value):
    return lax.ppermute(value, "c", [(0, 1), (1, 0)])


def all_to_all(value, axes):
    return lax.all_to_all(value, axes, 0, 0, tiled=True)


def two_parts(value):
    high = value.astype(BF16)
    return high, (value - high.astype(F32)).astype(BF16)


def three_parts(value):
    high = value.astype(BF16)
    rest = value - high.astype(F32)
    middle = rest.astype(BF16)
    return high, middle, (rest - middle.astype(F32)).astype(BF16)


def dot(left, right, dims=(((1,), (0,)), ((), ()))):
    return lax.dot_general(left, right, dims, preferred_element_type=F32)


def one_hot(count, numbers):
    rows = lax.broadcasted_iota(jnp.int32, (count, numbers.shape[1]), 0)
    return jnp.where(rows == numbers, 1.0, 0.0).astype(BF16)


def index_tile(index_ref, step, line, kind):
    at = pl.multiple_of((2 * line + kind) * LANES, LANES)
    tiles = index_ref[:, pl.ds(at, LANES)]
    return jnp.where(step == 0, tiles[0:1], tiles[1:2])


def pick_kernel(owners, points_ref, index_ref, keep_ref, send_ref):
    features, count = points_ref.shape
    steps = index_ref.shape[0]
    core, line = lax.axis_index("c"), lax.axis_index("x")
    numbers = [
        index_tile(index_ref, step, line, kind)
        for kind in (core, 1 - core)
        for step in range(steps)
    ]
    picked = dot(points_ref[...], one_hot(count, jnp.concatenate(numbers, axis=1)))
    empty = jnp.zeros((FEATURE_ROWS - features, picked.shape[1]), F32)
    picked = jnp.concatenate([picked, empty], axis=0).astype(BF16)
    for place, ref in enumerate((keep_ref, send_ref)):
        for step in range(steps):
            at = (place * steps + step) * LANES
            ref[step] = picked[:, at : at + LANES]


def pick_blocks(owners, points, index):
    shape = ((index.shape[0], FEATURE_ROWS, LANES), BF16)
    return call(pick_kernel, "pick_blocks", [shape, shape], owners, points.T, index)


def kernel_kernel(
    foreign,
    owners,
    points_ref,
    weights_ref,
    targets_ref,
    index_ref,
    blocks_ref,
    grad_ref,
    high_ref,
    low_ref,
    parts,
    norms,
):
    count, features = points_ref.shape
    outs = weights_ref.shape[0]
    pairs = blocks_ref.shape[0] // 2
    steps = index_ref.shape[0]
    gamma = 2.0 / features
    high, low = two_parts(weights_ref[...])
    parts[:outs, :] = high
    parts[outs:, :] = low
    for at in range(0, count, CHUNK):
        wide = points_ref[at : at + CHUNK, :].astype(F32)
        norms[at : at + CHUNK, :] = gamma * jnp.sum(wide * wide, axis=1, keepdims=True)

    blocks, block_norms, grads = [], [], []
    for step in range(steps):
        rows = slice(step * FEATURE_ROWS, (step + 1) * FEATURE_ROWS)
        for pair in range(pairs):
            block = jnp.concatenate(
                [blocks_ref[2 * pair, rows, :], blocks_ref[2 * pair + 1, rows, :]], axis=1
            )
            wide = block.astype(F32)
            blocks.append(block[:features, :])
            block_norms.append(gamma * jnp.sum(wide * wide, axis=0, keepdims=True))
            grads.append(jnp.zeros((outs, 2 * LANES), F32))

    units = [(n, at) for n in range(steps * pairs) for at in range(0, count, UNIT)]

    def cross(n, at):
        return dot(points_ref[at : at + UNIT, :], blocks[n])

    ahead = cross(*units[0])
    for place, (n, at) in enumerate(units):
        now = ahead
        if place + 1 < len(units):
            ahead = cross(*units[place + 1])
        rows = slice(at, at + UNIT)
        kern = jnp.exp((2.0 * gamma) * now - (norms[rows, :] + block_norms[n]))
        high, low = two_parts(kern)
        high_ref[n, rows, :] = high
        low_ref[n, rows, :] = low
        both = dot(parts[:, rows], high)
        grads[n] += both[:outs] + both[outs:] + dot(parts[:outs, rows], low)

    def tiles(n):
        step, pair = divmod(n, pairs)
        return [(step * pairs + pair) * 2 + k for k in range(2)]

    for n, grad in enumerate(grads):
        for k, tile in enumerate(tiles(n)):
            part = grad[:, k * LANES : (k + 1) * LANES]
            grad_ref[:, tile : tile + 1, :] = part.reshape(outs, 1, LANES)

    rank = my_rank()
    kind = lax.axis_index("c") ^ foreign
    for step in range(steps):

        @pl.when(owners[step] == rank)
        def _():
            own = three_parts(LAMBDA * weights_ref[...] - targets_ref[...])
            for line in range(2 * pairs):
                pick = one_hot(count, index_tile(index_ref, step, line, kind))
                terms = [dot(part, pick) for part in own]
                tile = step * 2 * pairs + line
                grad_ref[:, tile : tile + 1, :] += (
                    terms[0] + (terms[1] + terms[2])
                ).reshape(outs, 1, LANES)


def kernel_and_gradient(foreign, owners, points, weights, targets, index, blocks):
    count = points.shape[0]
    outs = weights.shape[0]
    tiles = index.shape[0] * blocks.shape[0]
    kern = ((tiles // 2, count, 2 * LANES), BF16)
    return call(
        functools.partial(kernel_kernel, foreign),
        "kernel_and_gradient",
        [((outs, tiles, LANES), F32), kern, kern],
        owners,
        points,
        weights,
        targets,
        index,
        blocks,
        scratch=[pltpu.VMEM((2 * outs, count), BF16), pltpu.VMEM((count, 1), F32)],
        cost=pl.CostEstimate(
            flops=tiles * LANES * count * (2 * FEATURE_ROWS + 6 * outs),
            bytes_accessed=4 * tiles * LANES * count,
            transcendentals=tiles * LANES * count,
        ),
    )


def between_kernel(features, owners, index_ref, own_ref, other_ref, out_ref):
    lines = own_ref.shape[0]
    gamma = 2.0 / features
    core = lax.axis_index("c")

    def tile(step, line, kind):
        at = step * FEATURE_ROWS
        rows = slice(at, at + FEATURE_ROWS)
        return jnp.where(core == kind, own_ref[line, rows, :], other_ref[line, rows, :])

    places = [(line, kind) for line in range(lines) for kind in range(2)]
    second = jnp.concatenate([tile(1, *place) for place in places], axis=1)
    wide = second.astype(F32)
    second_norm = gamma * jnp.sum(wide * wide, axis=0, keepdims=True)
    second_index = index_ref[1:2, :]
    extra = jnp.where(owners[0] == owners[1], LAMBDA, 0.0)
    for n, place in enumerate(places):
        first = tile(0, *place)
        wide = first.astype(F32)
        square = jnp.sum(wide * wide, axis=0, keepdims=True)
        first_norm = gamma * jnp.transpose(jnp.broadcast_to(square, (LANES, LANES)))[:, :1]
        first_index = jnp.transpose(
            jnp.broadcast_to(
                index_ref[0:1, n * LANES : (n + 1) * LANES].astype(F32), (LANES, LANES)
            )
        )[:, :1].astype(jnp.int32)
        cross = dot(first, second, FIRST_DIMS)
        kern = jnp.exp((2.0 * gamma) * cross - (first_norm + second_norm))
        out_ref[n * LANES : (n + 1) * LANES, :] = kern + jnp.where(
            first_index == second_index, extra, 0.0
        )


def between_blocks(features, owners, index, own, other):
    block = index.shape[1]
    return call(
        functools.partial(between_kernel, features),
        "between_blocks",
        [((block, block), F32)],
        owners,
        index,
        own,
        other,
        cost=pl.CostEstimate(
            flops=2 * block * block * FEATURE_ROWS,
            bytes_accessed=4 * block * block,
            transcendentals=block * block,
        ),
    )[0]


def chain_kernel(owners, mine_ref, theirs_ref, given_ref, between_ref, out_ref, grads):
    tiles = out_ref.shape[1]
    block = between_ref.shape[0]
    rows = given_ref.shape[2]
    lines = tiles // 2
    core = lax.axis_index("c")
    for step in range(2):
        for line in range(lines):
            at = slice(step * lines + line, step * lines + line + 1)
            for kind in range(2):
                lanes = slice((2 * line + kind) * LANES, (2 * line + kind + 1) * LANES)
                grads[step : step + 1, lanes] = jnp.where(
                    core == kind, theirs_ref[at, :], mine_ref[at, :]
                )

    diagonal = lax.broadcasted_iota(jnp.int32, (LANES, LANES), 0) == lax.broadcasted_iota(
        jnp.int32, (LANES, LANES), 1
    )
    share = LANES // rows
    correction = jnp.zeros((8, block), F32)
    for step in range(2):
        grad = grads[step : step + 1, :]
        if step == 1:
            grad = grad - jnp.sum(correction, axis=0, keepdims=True)
        for n in range(tiles):
            given = given_ref[n * share : (n + 1) * share, step].reshape(LANES, block)
            delta = jnp.sum(given * grad, axis=1, keepdims=True)
            row = jnp.sum(jnp.where(diagonal, delta, 0.0), axis=0, keepdims=True)
            out_ref[step, n : n + 1, :] = row
            if step == 0:
                product = delta * between_ref[n * LANES : (n + 1) * LANES, :]
                correction += jnp.sum(product.reshape(-1, 8, block), axis=0)


def run_chain(owners, mine, theirs, given, between):
    block = given.shape[3]
    return call(
        chain_kernel,
        "run_chain",
        [((2, block // LANES, LANES), F32)],
        owners,
        mine,
        theirs,
        given,
        between,
        scratch=[pltpu.VMEM((2, block), F32)],
    )[0]


def update_kernel(
    foreign,
    owners,
    delta_ref,
    index_ref,
    weights_ref,
    fitted_ref,
    own_high,
    own_low,
    other_high,
    other_low,
    new_weights_ref,
    new_fitted_ref,
):
    core = lax.axis_index("c")
    step = core ^ foreign
    outs, count = weights_ref.shape
    pairs = own_high.shape[0] // 2

    deltas = []
    for pair in range(pairs):
        for kind in (core, 1 - core):
            tiles = [
                delta_ref[:, pl.ds(2 * (2 * pair + k) + kind, 1), :].reshape(outs, LANES)
                for k in range(2)
            ]
            deltas.append((pair, kind, jnp.concatenate(tiles, axis=1)))
    parts = [two_parts(delta) for _, _, delta in deltas]
    both = [jnp.concatenate(part, axis=0) for part in parts]
    for at in range(0, count, CHUNK):
        rows = slice(at, at + CHUNK)
        total = jnp.zeros((2 * outs, CHUNK), F32)
        small = jnp.zeros((outs, CHUNK), F32)
        for n, (pair, _, _) in enumerate(deltas):
            high_ref, low_ref = ((own_high, own_low), (other_high, other_low))[n % 2]
            total += dot(both[n], high_ref[step * pairs + pair, rows, :], TRANSPOSED)
            small += dot(parts[n][0], low_ref[step * pairs + pair, rows, :], TRANSPOSED)
        new_fitted_ref[:, rows] = fitted_ref[:, rows] - (
            total[:outs] + (total[outs:] + small)
        )

    new_weights_ref[...] = weights_ref[...]

    @pl.when(owners[step] == my_rank())
    def _():
        for pair, kind, delta in deltas:
            numbers = [index_tile(index_ref, step, 2 * pair + k, kind) for k in range(2)]
            pick = one_hot(count, jnp.concatenate(numbers, axis=1))
            terms = [dot(part, pick, TRANSPOSED) for part in three_parts(delta)]
            new_weights_ref[...] -= terms[0] + (terms[1] + terms[2])


def update(foreign, owners, delta, index, weights, fitted, own, other):
    shape = (weights.shape, F32)
    return call(
        functools.partial(update_kernel, foreign),
        "update",
        [shape, shape],
        owners,
        delta,
        index,
        weights,
        fitted,
        *own,
        *other,
        cost=pl.CostEstimate(
            flops=6 * own[0].size * weights.shape[0],
            bytes_accessed=4 * own[0].size,
            transcendentals=0,
        ),
    )


def local(points, weights, targets, fitted, preconditioner, owners, block_index):
    steps = block_index.shape[0]
    features = points.shape[1]
    groups = GRID[0] * GRID[1]
    lines = lax.axis_size("x")
    core = lax.axis_index("c")
    per_step = (groups // steps).bit_length() - 1

    given = lax.all_gather(preconditioner, DP, axis=0)

    keep, send = pick_blocks(owners, points, block_index)
    got = exchange(send)
    owner_core = (owners & 1).reshape(steps, 1, 1)
    parcels = jnp.where(owner_core == core, keep, got)
    parcels = all_to_all(parcels.reshape(groups, -1, LANES), ZY)
    late = lax.axis_index(ZY) >> per_step
    holder = (jnp.where(late == 0, owners[0], owners[1]) >> 1).astype(jnp.uint32)
    zero = jnp.uint32(0)
    piece = lax.dynamic_slice(parcels, (holder, zero, zero), (1, *parcels.shape[1:]))
    blocks = all_to_all(jnp.broadcast_to(piece, parcels.shape), ZY)
    blocks = blocks.reshape(1, steps * FEATURE_ROWS, LANES)
    own = all_to_all(jnp.broadcast_to(blocks, (lines, *blocks.shape[1:])), "x")
    other = exchange(own)

    data = (points, weights, targets, block_index)
    grad_own, *kern_own = kernel_and_gradient(0, owners, *data, own)
    grad_theirs = exchange(grad_own)
    grad_other, *kern_other = kernel_and_gradient(1, owners, *data, other)
    grad = all_to_all(grad_other + grad_theirs, ZY)
    grad = jnp.sum(grad, axis=0)
    between = between_blocks(features, owners, block_index, own, other)
    grad, between = lax.optimization_barrier((grad, between))
    delta = run_chain(owners, grad, exchange(grad), given, between)

    mine = jnp.where(core == 0, delta[0], delta[1])[None]
    mine = all_to_all(jnp.broadcast_to(mine, (groups, *mine.shape[1:])), ZY)
    theirs = exchange(mine)
    rest = (kern_own, kern_other)
    weights, fitted = update(0, owners, mine, block_index, weights, fitted, *rest)
    weights, fitted = update(1, owners, theirs, block_index, weights, fitted, *rest)
    return (weights, fitted)


def solution(mesh):
    grid = Mesh(mesh.devices.reshape(*GRID, mesh.shape["out"]), (*DP, "x"))
    return jax.shard_map(
        local,
        mesh=grid,
        in_specs=(
            P(DP, None),
            P("x", DP),
            P("x", DP),
            P("x", DP),
            P(None, DP, None),
            P(),
            P(),
        ),
        out_specs=(P("x", DP), P("x", DP)),
        check_vma=False,
    )
```

```python
import functools

import jax
import jax.numpy as jnp
from jax import lax
from jax.experimental import pallas as pl
from jax.experimental.pallas import tpu as pltpu
from jax.sharding import Mesh, PartitionSpec as P

LAMBDA = 0.5
GRID = (8, 8, 2)
ZY = ("z", "y")
DP = ("z", "y", "c")
FEATURE_ROWS = 512
LANES = 128
CHUNK = 256
UNIT = 768
VMEM_BYTES = 16 * 1024 * 1024
BF16 = jnp.bfloat16
F32 = jnp.float32
TRANSPOSED = (((1,), (1,)), ((), ()))
FIRST_DIMS = (((0,), (0,)), ((), ()))
WHOLE = pl.BlockSpec(memory_space=pltpu.VMEM)


def call(
    kernel,
    name,
    shapes,
    owners,
    *args,
    scratch=(),
    cost=None,
):
    return pl.pallas_call(
        kernel,
        grid_spec=pltpu.PrefetchScalarGridSpec(
            num_scalar_prefetch=1,
            grid=(),
            in_specs=[WHOLE] * len(args),
            out_specs=[WHOLE] * len(shapes),
            scratch_shapes=list(scratch),
        ),
        out_shape=[jax.ShapeDtypeStruct(*shape) for shape in shapes],
        compiler_params=pltpu.CompilerParams(vmem_limit_bytes=VMEM_BYTES),
        cost_estimate=cost,
        name=name,
    )(owners, *args)


def my_rank():
    return (lax.axis_index("z") * GRID[1] + lax.axis_index("y")) * GRID[2] + lax.axis_index("c")


def exchange(value):
    return lax.ppermute(value, "c", [(0, 1), (1, 0)])


def all_to_all(value, axes):
    return lax.all_to_all(value, axes, 0, 0, tiled=True)


def two_parts(value):
    high = value.astype(BF16)
    return high, (value - high.astype(F32)).astype(BF16)


def three_parts(value):
    high = value.astype(BF16)
    rest = value - high.astype(F32)
    middle = rest.astype(BF16)
    return high, middle, (rest - middle.astype(F32)).astype(BF16)


def dot(left, right, dims=(((1,), (0,)), ((), ()))):
    return lax.dot_general(left, right, dims, preferred_element_type=F32)


def exact_dot(value, pick, dims=(((1,), (0,)), ((), ()))):
    rows = value.shape[0]
    terms = dot(jnp.concatenate(three_parts(value), axis=0), pick, dims)
    return terms[:rows] + (terms[rows : 2 * rows] + terms[2 * rows :])


def one_hot(count, numbers):
    rows = lax.broadcasted_iota(jnp.int32, (count, numbers.shape[1]), 0)
    return jnp.where(rows == numbers, 1.0, 0.0).astype(BF16)


def index_tile(index_ref, step, line, kind):
    at = pl.multiple_of((2 * line + kind) * LANES, LANES)
    tiles = index_ref[:, pl.ds(at, LANES)]
    return jnp.where(step == 0, tiles[0:1], tiles[1:2])


def pick_kernel(points_ref, index_ref, keep_ref, send_ref):
    features, count = points_ref.shape
    steps = index_ref.shape[0]
    core, line = lax.axis_index("c"), lax.axis_index("x")
    numbers = [
        index_tile(index_ref, step, line, kind)
        for kind in (core, 1 - core)
        for step in range(steps)
    ]
    picked = dot(points_ref[...], one_hot(count, jnp.concatenate(numbers, axis=1)))
    empty = jnp.zeros((FEATURE_ROWS - features, picked.shape[1]), F32)
    picked = jnp.concatenate([picked, empty], axis=0).astype(BF16)
    for place, ref in enumerate((keep_ref, send_ref)):
        for step in range(steps):
            at = (place * steps + step) * LANES
            ref[step] = picked[:, at : at + LANES]


def pick_blocks(points, index):
    shape = jax.ShapeDtypeStruct((index.shape[0], FEATURE_ROWS, LANES), BF16)
    block = pl.BlockSpec(shape.shape, lambda i: (0, 0, 0))
    return pl.pallas_call(
        pick_kernel,
        grid=(1,),
        in_specs=[pl.BlockSpec(array.shape, lambda i: (0, 0)) for array in (points, index)],
        out_specs=[block, block],
        out_shape=[shape, shape],
        compiler_params=pltpu.CompilerParams(vmem_limit_bytes=VMEM_BYTES),
        name="pick_blocks",
    )(points, index)


def choose_kernel(owners, keep_ref, got_ref, out_ref):
    core = lax.axis_index("c")
    for step in range(out_ref.shape[0]):
        mine = (owners[step] & 1) == core
        out_ref[step] = jnp.where(mine, keep_ref[step], got_ref[step])


def choose(owners, keep, got):
    return call(choose_kernel, "choose", [(keep.shape, BF16)], owners, keep, got)[0]


def take_kernel(owners, parcels_ref, out_ref):
    groups = parcels_ref.shape[0]
    per_step = groups // owners.shape[0]
    zy = lax.axis_index("z") * GRID[1] + lax.axis_index("y")
    holder = jnp.where(zy < per_step, owners[0], owners[1]) >> 1
    piece = parcels_ref[pl.ds(holder, 1)]
    out_ref[...] = jnp.broadcast_to(piece, out_ref.shape)


def take(owners, parcels):
    return call(take_kernel, "take", [(parcels.shape, BF16)], owners, parcels)[0]


def prepare(features, points_ref, weights_ref, rows_ref, norms_ref, parts_ref):
    count = points_ref.shape[1]
    outs = weights_ref.shape[0]
    gamma = 2.0 / features
    empty = jnp.zeros((FEATURE_ROWS - features, LANES), F32)
    for at in range(0, count, LANES):
        rows = slice(at, at + LANES)
        wide = jnp.concatenate([points_ref[:, rows].astype(F32), empty], axis=0)
        wide = jnp.transpose(wide)
        rows_ref[rows, :] = wide.astype(BF16)
        norms_ref[rows, :] = gamma * jnp.sum(wide * wide, axis=1, keepdims=True)
    high, low = two_parts(weights_ref[...])
    parts_ref[:outs, :] = high
    parts_ref[outs:, :] = low


def kernel_body(
    features,
    foreign,
    owners,
    rows_ref,
    norms_ref,
    parts_ref,
    weights_ref,
    targets_ref,
    index_ref,
    blocks_ref,
    grad_ref,
    high_ref,
    low_ref,
):
    count = rows_ref.shape[0]
    outs = weights_ref.shape[0]
    pairs = blocks_ref.shape[0] // 2
    steps = index_ref.shape[0]
    gamma = 2.0 / features

    blocks, block_norms, grads = [], [], []
    for step in range(steps):
        rows = slice(step * FEATURE_ROWS, (step + 1) * FEATURE_ROWS)
        for pair in range(pairs):
            block = jnp.concatenate(
                [blocks_ref[2 * pair, rows, :], blocks_ref[2 * pair + 1, rows, :]], axis=1
            )
            wide = block.astype(F32)
            blocks.append(block)
            block_norms.append(gamma * jnp.sum(wide * wide, axis=0, keepdims=True))
            grads.append(jnp.zeros((outs, 2 * LANES), F32))

    units = [(n, at) for n in range(steps * pairs) for at in range(0, count, UNIT)]

    def cross(n, at):
        return dot(rows_ref[at : at + UNIT, :], blocks[n])

    ahead = cross(*units[0])
    for place, (n, at) in enumerate(units):
        now = ahead
        if place + 1 < len(units):
            ahead = cross(*units[place + 1])
        rows = slice(at, at + UNIT)
        kern = jnp.exp((2.0 * gamma) * now - (norms_ref[rows, :] + block_norms[n]))
        high, low = two_parts(kern)
        high_ref[n, rows, :] = high
        low_ref[n, rows, :] = low
        both = dot(parts_ref[:, rows], high)
        grads[n] += both[:outs] + both[outs:] + dot(parts_ref[:outs, rows], low)

    for n, grad in enumerate(grads):
        for k in range(2):
            tile = 2 * n + k
            part = grad[:, k * LANES : (k + 1) * LANES]
            grad_ref[:, tile : tile + 1, :] = part.reshape(outs, 1, LANES)

    rank = my_rank()
    kind = lax.axis_index("c") ^ foreign
    for step in range(steps):

        @pl.when(owners[step] == rank)
        def _():
            own = LAMBDA * weights_ref[...] - targets_ref[...]
            for pair in range(pairs):
                numbers = [index_tile(index_ref, step, 2 * pair + k, kind) for k in range(2)]
                term = exact_dot(own, one_hot(count, jnp.concatenate(numbers, axis=1)))
                for k in range(2):
                    tile = (step * pairs + pair) * 2 + k
                    part = term[:, k * LANES : (k + 1) * LANES]
                    grad_ref[:, tile : tile + 1, :] += part.reshape(outs, 1, LANES)


def first_kernel(features, owners, points, weights, targets, index, blocks, *rest):
    grad, high, low, rows, norms, parts = rest
    prepare(features, points, weights, rows, norms, parts)
    kernel_body(
        features, 0, owners, rows, norms, parts, weights, targets, index, blocks,
        grad, high, low,
    )


def second_kernel(features, *refs):
    kernel_body(features, 1, *refs)


def kernel_and_gradient(features, owners, data, weights, targets, index, blocks, first):
    outs, count = weights.shape
    tiles = index.shape[0] * blocks.shape[0]
    kern = (tiles // 2, count, 2 * LANES)
    shapes = [((outs, tiles, LANES), F32), (kern, BF16), (kern, BF16)]
    if first:
        shapes += [((count, FEATURE_ROWS), BF16), ((count, 1), F32), ((2 * outs, count), BF16)]
    return call(
        functools.partial(first_kernel if first else second_kernel, features),
        "first_half" if first else "second_half",
        shapes,
        owners,
        *data,
        weights,
        targets,
        index,
        blocks,
        cost=pl.CostEstimate(
            flops=tiles * LANES * count * (2 * FEATURE_ROWS + 6 * outs),
            bytes_accessed=4 * tiles * LANES * count,
            transcendentals=tiles * LANES * count,
        ),
    )


def between_kernel(features, owners, index_ref, own_ref, other_ref, out_ref):
    lines = own_ref.shape[0]
    gamma = 2.0 / features
    core = lax.axis_index("c")

    def tile(step, line, kind):
        at = step * FEATURE_ROWS
        rows = slice(at, at + FEATURE_ROWS)
        return jnp.where(core == kind, own_ref[line, rows, :], other_ref[line, rows, :])

    places = [(line, kind) for line in range(lines) for kind in range(2)]
    second = jnp.concatenate([tile(1, *place) for place in places], axis=1)
    wide = second.astype(F32)
    second_norm = gamma * jnp.sum(wide * wide, axis=0, keepdims=True)
    second_index = index_ref[1:2, :]
    extra = jnp.where(owners[0] == owners[1], LAMBDA, 0.0)
    for n, place in enumerate(places):
        first = tile(0, *place)
        wide = first.astype(F32)
        square = jnp.sum(wide * wide, axis=0, keepdims=True)
        first_norm = gamma * jnp.transpose(jnp.broadcast_to(square, (LANES, LANES)))[:, :1]
        first_index = jnp.transpose(
            jnp.broadcast_to(
                index_ref[0:1, n * LANES : (n + 1) * LANES].astype(F32), (LANES, LANES)
            )
        )[:, :1].astype(jnp.int32)
        cross = dot(first, second, FIRST_DIMS)
        kern = jnp.exp((2.0 * gamma) * cross - (first_norm + second_norm))
        out_ref[n * LANES : (n + 1) * LANES, :] = kern + jnp.where(
            first_index == second_index, extra, 0.0
        )


def between_blocks(features, owners, index, own, other):
    block = index.shape[1]
    return call(
        functools.partial(between_kernel, features),
        "between_blocks",
        [((block, block), F32)],
        owners,
        index,
        own,
        other,
        cost=pl.CostEstimate(
            flops=2 * block * block * FEATURE_ROWS,
            bytes_accessed=4 * block * block,
            transcendentals=block * block,
        ),
    )[0]


def chain_kernel(owners, mine_ref, theirs_ref, given_ref, between_ref, out_ref, grads):
    tiles = out_ref.shape[0]
    block = between_ref.shape[0]
    rows = given_ref.shape[2]
    lines = tiles // 2
    core = lax.axis_index("c")
    for step in range(2):
        for line in range(lines):
            at = slice(step * lines + line, step * lines + line + 1)
            for kind in range(2):
                lanes = slice((2 * line + kind) * LANES, (2 * line + kind + 1) * LANES)
                grads[step : step + 1, lanes] = jnp.where(
                    core == kind, theirs_ref[at, :], mine_ref[at, :]
                )

    diagonal = lax.broadcasted_iota(jnp.int32, (LANES, LANES), 0) == lax.broadcasted_iota(
        jnp.int32, (LANES, LANES), 1
    )
    share = LANES // rows
    correction = jnp.zeros((8, block), F32)
    for step in range(2):
        grad = grads[step : step + 1, :]
        if step == 1:
            grad = grad - jnp.sum(correction, axis=0, keepdims=True)
        for n in range(tiles):
            given = given_ref[n * share : (n + 1) * share, step].reshape(LANES, block)
            delta = jnp.sum(given * grad, axis=1, keepdims=True)
            row = jnp.sum(jnp.where(diagonal, delta, 0.0), axis=0, keepdims=True)
            if step == 0:
                out_ref[n : n + 1, :] = row
            else:
                out_ref[n : n + 1, :] = jnp.where(core == 0, out_ref[n : n + 1, :], row)
            if step == 0:
                product = delta * between_ref[n * LANES : (n + 1) * LANES, :]
                correction += jnp.sum(product.reshape(-1, 8, block), axis=0)


def run_chain(owners, mine, theirs, given, between):
    block = given.shape[3]
    return call(
        chain_kernel,
        "run_chain",
        [((block // LANES, LANES), F32)],
        owners,
        mine,
        theirs,
        given,
        between,
        scratch=[pltpu.VMEM((2, block), F32)],
    )[0]


def update_kernel(
    foreign,
    owners,
    delta_ref,
    index_ref,
    weights_ref,
    fitted_ref,
    own_high,
    own_low,
    other_high,
    other_low,
    new_weights_ref,
    new_fitted_ref,
):
    core = lax.axis_index("c")
    step = core ^ foreign
    outs, count = weights_ref.shape
    pairs = own_high.shape[0] // 2

    deltas = []
    for pair in range(pairs):
        for kind in (core, 1 - core):
            tiles = [
                delta_ref[:, pl.ds(2 * (2 * pair + k) + kind, 1), :].reshape(outs, LANES)
                for k in range(2)
            ]
            deltas.append((pair, kind, jnp.concatenate(tiles, axis=1)))
    parts = [two_parts(delta) for _, _, delta in deltas]
    both = [jnp.concatenate(part, axis=0) for part in parts]
    for at in range(0, count, CHUNK):
        rows = slice(at, at + CHUNK)
        total = jnp.zeros((2 * outs, CHUNK), F32)
        small = jnp.zeros((outs, CHUNK), F32)
        for n, (pair, _, _) in enumerate(deltas):
            high_ref, low_ref = ((own_high, own_low), (other_high, other_low))[n % 2]
            total += dot(both[n], high_ref[step * pairs + pair, rows, :], TRANSPOSED)
            small += dot(parts[n][0], low_ref[step * pairs + pair, rows, :], TRANSPOSED)
        new_fitted_ref[:, rows] = fitted_ref[:, rows] - (
            total[:outs] + (total[outs:] + small)
        )

    new_weights_ref[...] = weights_ref[...]

    @pl.when(owners[step] == my_rank())
    def _():
        for pair, kind, delta in deltas:
            numbers = [index_tile(index_ref, step, 2 * pair + k, kind) for k in range(2)]
            pick = one_hot(count, jnp.concatenate(numbers, axis=1))
            new_weights_ref[...] -= exact_dot(delta, pick, TRANSPOSED)


def update(foreign, owners, delta, index, weights, fitted, own, other):
    shape = (weights.shape, F32)
    return call(
        functools.partial(update_kernel, foreign),
        "update",
        [shape, shape],
        owners,
        delta,
        index,
        weights,
        fitted,
        *own,
        *other,
        cost=pl.CostEstimate(
            flops=6 * own[0].size * weights.shape[0],
            bytes_accessed=4 * own[0].size,
            transcendentals=0,
        ),
    )


def local(points, weights, targets, fitted, preconditioner, owners, block_index):
    steps = block_index.shape[0]
    features = points.shape[1]
    groups = GRID[0] * GRID[1]
    lines = lax.axis_size("x")

    given = lax.all_gather(preconditioner, DP, axis=0)

    keep, send = pick_blocks(points.T, block_index)
    parcels = choose(owners, keep, exchange(send)).reshape(groups, -1, LANES)
    blocks = all_to_all(take(owners, all_to_all(parcels, ZY)), ZY)
    blocks = blocks.reshape(1, steps * FEATURE_ROWS, LANES)
    own = all_to_all(jnp.broadcast_to(blocks, (lines, *blocks.shape[1:])), "x")
    other = exchange(own)

    data = (weights, targets, block_index)
    grad_own, *kern_own, rows, norms, parts = kernel_and_gradient(
        features, owners, (points.T,), *data, own, True
    )
    grad_theirs = exchange(grad_own)
    grad_other, *kern_other = kernel_and_gradient(
        features, owners, (rows, norms, parts), *data, other, False
    )
    grad = all_to_all(grad_other + grad_theirs, ZY)
    grad, given, own, other = lax.optimization_barrier((grad, given, own, other))
    grad = jnp.sum(grad, axis=0)
    theirs = exchange(grad)
    between = between_blocks(features, owners, block_index, own, other)
    mine = run_chain(owners, grad, theirs, given, between)

    mine = all_to_all(jnp.broadcast_to(mine, (groups, *mine.shape)), ZY)
    theirs = exchange(mine)
    rest = (kern_own, kern_other)
    weights, fitted = update(0, owners, mine, block_index, weights, fitted, *rest)
    weights, fitted = update(1, owners, theirs, block_index, weights, fitted, *rest)
    return (weights, fitted)


def solution(mesh):
    grid = Mesh(mesh.devices.reshape(*GRID, mesh.shape["out"]), (*DP, "x"))
    return jax.shard_map(
        local,
        mesh=grid,
        in_specs=(
            P(DP, None),
            P("x", DP),
            P("x", DP),
            P("x", DP),
            P(None, DP, None),
            P(),
            P(),
        ),
        out_specs=(P("x", DP), P("x", DP)),
        check_vma=False,
    )
```

```python
import functools

import jax
import jax.numpy as jnp
from jax import lax
from jax.experimental import pallas as pl
from jax.experimental.pallas import tpu as pltpu
from jax.sharding import Mesh, PartitionSpec as P

LAMBDA = 0.5
GRID = (8, 8, 2)
ZY = ("z", "y")
DP = ("z", "y", "c")
FEATURE_ROWS = 512
KEPT_ROWS = 448
LANES = 128
CHUNK = 256
UNIT = 768
SHARE = 16
VMEM_BYTES = 16 * 1024 * 1024
BETWEEN_BYTES = 36 * 1024 * 1024
BF16 = jnp.bfloat16
F32 = jnp.float32
TRANSPOSED = (((1,), (1,)), ((), ()))
FIRST_DIMS = (((0,), (0,)), ((), ()))
WHOLE = pl.BlockSpec(memory_space=pltpu.VMEM)
FAR = pl.BlockSpec(memory_space=pltpu.HBM)


def call(
    kernel,
    name,
    shapes,
    owners,
    *args,
    in_specs=None,
    scratch=(),
    cost=None,
    vmem=VMEM_BYTES,
):
    return pl.pallas_call(
        kernel,
        grid_spec=pltpu.PrefetchScalarGridSpec(
            num_scalar_prefetch=1,
            grid=(),
            in_specs=in_specs or [WHOLE] * len(args),
            out_specs=[WHOLE] * len(shapes),
            scratch_shapes=list(scratch),
        ),
        out_shape=[jax.ShapeDtypeStruct(*shape) for shape in shapes],
        compiler_params=pltpu.CompilerParams(vmem_limit_bytes=vmem),
        cost_estimate=cost,
        name=name,
    )(owners, *args)


def my_rank():
    return (lax.axis_index("z") * GRID[1] + lax.axis_index("y")) * GRID[2] + lax.axis_index("c")


def exchange(value):
    return lax.ppermute(value, "c", [(0, 1), (1, 0)])


def all_to_all(value, axes):
    return lax.all_to_all(value, axes, 0, 0, tiled=True)


def two_parts(value):
    high = value.astype(BF16)
    return high, (value - high.astype(F32)).astype(BF16)


def three_parts(value):
    high = value.astype(BF16)
    rest = value - high.astype(F32)
    middle = rest.astype(BF16)
    return high, middle, (rest - middle.astype(F32)).astype(BF16)


def dot(left, right, dims=(((1,), (0,)), ((), ()))):
    return lax.dot_general(left, right, dims, preferred_element_type=F32)


def exact_dot(value, pick, dims=(((1,), (0,)), ((), ()))):
    rows = value.shape[0]
    terms = dot(jnp.concatenate(three_parts(value), axis=0), pick, dims)
    return terms[:rows] + (terms[rows : 2 * rows] + terms[2 * rows :])


def one_hot(count, numbers):
    rows = lax.broadcasted_iota(jnp.int32, (count, numbers.shape[1]), 0)
    return jnp.where(rows == numbers, 1.0, 0.0).astype(BF16)


def index_tile(index_ref, step, line, kind):
    at = pl.multiple_of((2 * line + kind) * LANES, LANES)
    tiles = index_ref[:, pl.ds(at, LANES)]
    return jnp.where(step == 0, tiles[0:1], tiles[1:2])


def pick_kernel(points_ref, index_ref, keep_ref, send_ref):
    features, count = points_ref.shape
    steps = index_ref.shape[0]
    core, line = lax.axis_index("c"), lax.axis_index("x")
    numbers = [
        index_tile(index_ref, step, line, kind)
        for kind in (core, 1 - core)
        for step in range(steps)
    ]
    picked = dot(points_ref[...], one_hot(count, jnp.concatenate(numbers, axis=1)))
    empty = jnp.zeros((FEATURE_ROWS - features, picked.shape[1]), F32)
    picked = jnp.concatenate([picked, empty], axis=0).astype(BF16)
    for place, ref in enumerate((keep_ref, send_ref)):
        for step in range(steps):
            at = (place * steps + step) * LANES
            ref[step] = picked[:, at : at + LANES]


def pick_blocks(points, index):
    shape = jax.ShapeDtypeStruct((index.shape[0], FEATURE_ROWS, LANES), BF16)
    block = pl.BlockSpec(shape.shape, lambda i: (0, 0, 0))
    return pl.pallas_call(
        pick_kernel,
        grid=(1,),
        in_specs=[pl.BlockSpec(array.shape, lambda i: (0, 0)) for array in (points, index)],
        out_specs=[block, block],
        out_shape=[shape, shape],
        compiler_params=pltpu.CompilerParams(vmem_limit_bytes=VMEM_BYTES),
        name="pick_blocks",
    )(points, index)


def choose_kernel(owners, keep_ref, got_ref, out_ref):
    core = lax.axis_index("c")
    for step in range(out_ref.shape[0]):
        mine = (owners[step] & 1) == core
        out_ref[step] = jnp.where(mine, keep_ref[step], got_ref[step])


def choose(owners, keep, got):
    return call(choose_kernel, "choose", [(keep.shape, BF16)], owners, keep, got)[0]


def take_kernel(owners, parcels_ref, out_ref):
    groups = parcels_ref.shape[0]
    per_step = groups // owners.shape[0]
    zy = lax.axis_index("z") * GRID[1] + lax.axis_index("y")
    holder = jnp.where(zy < per_step, owners[0], owners[1]) >> 1
    piece = parcels_ref[pl.ds(holder, 1)]
    out_ref[...] = jnp.broadcast_to(piece, out_ref.shape)


def take(owners, parcels):
    return call(take_kernel, "take", [(parcels.shape, BF16)], owners, parcels)[0]


def prepare(features, points_ref, weights_ref, rows_ref, norms_ref, parts_ref):
    count = points_ref.shape[1]
    outs = weights_ref.shape[0]
    gamma = 2.0 / features
    empty = jnp.zeros((KEPT_ROWS - features, LANES), F32)
    for at in range(0, count, LANES):
        rows = slice(at, at + LANES)
        wide = jnp.concatenate([points_ref[:, rows].astype(F32), empty], axis=0)
        wide = jnp.transpose(wide)
        rows_ref[rows, :] = wide.astype(BF16)
        norms_ref[rows, :] = gamma * jnp.sum(wide * wide, axis=1, keepdims=True)
    high, low = two_parts(weights_ref[...])
    parts_ref[:outs, :] = high
    parts_ref[outs:, :] = low


def kernel_body(
    features,
    foreign,
    owners,
    rows_ref,
    norms_ref,
    parts_ref,
    weights_ref,
    targets_ref,
    index_ref,
    blocks_ref,
    grad_ref,
    high_ref,
    low_ref,
):
    count = rows_ref.shape[0]
    outs = weights_ref.shape[0]
    pairs = blocks_ref.shape[0] // 2
    steps = index_ref.shape[0]
    gamma = 2.0 / features

    blocks, block_norms, grads = [], [], []
    for step in range(steps):
        rows = slice(step * KEPT_ROWS, (step + 1) * KEPT_ROWS)
        for pair in range(pairs):
            block = jnp.concatenate(
                [blocks_ref[2 * pair, rows, :], blocks_ref[2 * pair + 1, rows, :]], axis=1
            )
            wide = block.astype(F32)
            blocks.append(block)
            block_norms.append(gamma * jnp.sum(wide * wide, axis=0, keepdims=True))
            grads.append(jnp.zeros((outs, 2 * LANES), F32))

    units = [(n, at) for n in range(steps * pairs) for at in range(0, count, UNIT)]

    def cross(n, at):
        return dot(rows_ref[at : at + UNIT, :], blocks[n])

    ahead = cross(*units[0])
    for place, (n, at) in enumerate(units):
        now = ahead
        if place + 1 < len(units):
            ahead = cross(*units[place + 1])
        rows = slice(at, at + UNIT)
        kern = jnp.exp((2.0 * gamma) * now - (norms_ref[rows, :] + block_norms[n]))
        high, low = two_parts(kern)
        high_ref[n, rows, :] = high
        low_ref[n, rows, :] = low
        both = dot(parts_ref[:, rows], high)
        grads[n] += both[:outs] + both[outs:] + dot(parts_ref[:outs, rows], low)

    for n, grad in enumerate(grads):
        for k in range(2):
            tile = 2 * n + k
            part = grad[:, k * LANES : (k + 1) * LANES]
            grad_ref[:, tile : tile + 1, :] = part.reshape(outs, 1, LANES)

    rank = my_rank()
    kind = lax.axis_index("c") ^ foreign
    for step in range(steps):

        @pl.when(owners[step] == rank)
        def _():
            own = LAMBDA * weights_ref[...] - targets_ref[...]
            for pair in range(pairs):
                numbers = [index_tile(index_ref, step, 2 * pair + k, kind) for k in range(2)]
                term = exact_dot(own, one_hot(count, jnp.concatenate(numbers, axis=1)))
                for k in range(2):
                    tile = (step * pairs + pair) * 2 + k
                    part = term[:, k * LANES : (k + 1) * LANES]
                    grad_ref[:, tile : tile + 1, :] += part.reshape(outs, 1, LANES)


def first_kernel(features, owners, points, weights, targets, index, blocks, *rest):
    grad, high, low, rows, norms, parts = rest
    prepare(features, points, weights, rows, norms, parts)
    kernel_body(
        features, 0, owners, rows, norms, parts, weights, targets, index, blocks,
        grad, high, low,
    )


def second_kernel(features, *refs):
    kernel_body(features, 1, *refs)


def kernel_and_gradient(features, owners, data, weights, targets, index, blocks, first):
    outs, count = weights.shape
    tiles = index.shape[0] * blocks.shape[0]
    kern = (tiles // 2, count, 2 * LANES)
    shapes = [((outs, tiles, LANES), F32), (kern, BF16), (kern, BF16)]
    if first:
        shapes += [((count, KEPT_ROWS), BF16), ((count, 1), F32), ((2 * outs, count), BF16)]
    return call(
        functools.partial(first_kernel if first else second_kernel, features),
        "first_half" if first else "second_half",
        shapes,
        owners,
        *data,
        weights,
        targets,
        index,
        blocks,
        cost=pl.CostEstimate(
            flops=tiles * LANES * count * (2 * KEPT_ROWS + 6 * outs),
            bytes_accessed=4 * tiles * LANES * count,
            transcendentals=tiles * LANES * count,
        ),
    )


def between_kernel(
    features, owners, index_ref, own_ref, other_ref, given_far, out_ref, given_ref, sems
):
    copies = [
        pltpu.make_async_copy(given_far.at[rows], given_ref.at[rows], sems.at[n])
        for n, rows in enumerate(slice(at, at + SHARE) for at in range(0, given_ref.shape[0], SHARE))
    ]
    for copy in copies:
        copy.start()
    lines = own_ref.shape[0]
    gamma = 2.0 / features
    core = lax.axis_index("c")

    def tile(step, line, kind):
        at = step * KEPT_ROWS
        rows = slice(at, at + KEPT_ROWS)
        return jnp.where(core == kind, own_ref[line, rows, :], other_ref[line, rows, :])

    places = [(line, kind) for line in range(lines) for kind in range(2)]
    second = jnp.concatenate([tile(1, *place) for place in places], axis=1)
    wide = second.astype(F32)
    second_norm = gamma * jnp.sum(wide * wide, axis=0, keepdims=True)
    second_index = index_ref[1:2, :]
    extra = jnp.where(owners[0] == owners[1], LAMBDA, 0.0)
    for n, place in enumerate(places):
        first = tile(0, *place)
        wide = first.astype(F32)
        square = jnp.sum(wide * wide, axis=0, keepdims=True)
        first_norm = gamma * jnp.transpose(jnp.broadcast_to(square, (LANES, LANES)))[:, :1]
        first_index = jnp.transpose(
            jnp.broadcast_to(
                index_ref[0:1, n * LANES : (n + 1) * LANES].astype(F32), (LANES, LANES)
            )
        )[:, :1].astype(jnp.int32)
        cross = dot(first, second, FIRST_DIMS)
        kern = jnp.exp((2.0 * gamma) * cross - (first_norm + second_norm))
        out_ref[n * LANES : (n + 1) * LANES, :] = kern + jnp.where(
            first_index == second_index, extra, 0.0
        )
    for copy in copies:
        copy.wait()


def between_blocks(features, owners, index, own, other, given):
    block = index.shape[1]
    return call(
        functools.partial(between_kernel, features),
        "between_blocks",
        [((block, block), F32), (given.shape, F32)],
        owners,
        index,
        own,
        other,
        given,
        in_specs=[WHOLE] * 3 + [FAR],
        scratch=[pltpu.SemaphoreType.DMA((given.shape[0] // SHARE,))],
        cost=pl.CostEstimate(
            flops=2 * block * block * KEPT_ROWS,
            bytes_accessed=4 * block * block,
            transcendentals=block * block,
        ),
        vmem=BETWEEN_BYTES,
    )


def chain_kernel(owners, mine_ref, theirs_ref, given_ref, between_ref, out_ref, grads):
    tiles = out_ref.shape[0]
    block = between_ref.shape[0]
    rows = given_ref.shape[2]
    lines = tiles // 2
    core = lax.axis_index("c")
    for step in range(2):
        for line in range(lines):
            at = slice(step * lines + line, step * lines + line + 1)
            for kind in range(2):
                lanes = slice((2 * line + kind) * LANES, (2 * line + kind + 1) * LANES)
                grads[step : step + 1, lanes] = jnp.where(
                    core == kind, theirs_ref[at, :], mine_ref[at, :]
                )

    diagonal = lax.broadcasted_iota(jnp.int32, (LANES, LANES), 0) == lax.broadcasted_iota(
        jnp.int32, (LANES, LANES), 1
    )
    share = LANES // rows
    correction = jnp.zeros((8, block), F32)
    for step in range(2):
        grad = grads[step : step + 1, :]
        if step == 1:
            grad = grad - jnp.sum(correction, axis=0, keepdims=True)
        for n in range(tiles):
            given = given_ref[n * share : (n + 1) * share, step].reshape(LANES, block)
            delta = jnp.sum(given * grad, axis=1, keepdims=True)
            row = jnp.sum(jnp.where(diagonal, delta, 0.0), axis=0, keepdims=True)
            if step == 0:
                out_ref[n : n + 1, :] = row
            else:
                out_ref[n : n + 1, :] = jnp.where(core == 0, out_ref[n : n + 1, :], row)
            if step == 0:
                product = delta * between_ref[n * LANES : (n + 1) * LANES, :]
                correction += jnp.sum(product.reshape(-1, 8, block), axis=0)


def run_chain(owners, mine, theirs, given, between):
    block = given.shape[3]
    return call(
        chain_kernel,
        "run_chain",
        [((block // LANES, LANES), F32)],
        owners,
        mine,
        theirs,
        given,
        between,
        scratch=[pltpu.VMEM((2, block), F32)],
    )[0]


def total_kernel(owners, parts_ref, out_ref):
    total = parts_ref[0]
    for n in range(1, parts_ref.shape[0]):
        total += parts_ref[n]
    out_ref[...] = total


def total(owners, parts):
    return call(total_kernel, "total", [(parts.shape[1:], F32)], owners, parts)[0]


def update_kernel(
    foreign,
    owners,
    delta_ref,
    index_ref,
    weights_ref,
    fitted_ref,
    own_high,
    own_low,
    other_high,
    other_low,
    new_weights_ref,
    new_fitted_ref,
):
    core = lax.axis_index("c")
    step = core ^ foreign
    outs, count = weights_ref.shape
    pairs = own_high.shape[0] // 2

    deltas = []
    for pair in range(pairs):
        for kind in (core, 1 - core):
            tiles = [
                delta_ref[:, pl.ds(2 * (2 * pair + k) + kind, 1), :].reshape(outs, LANES)
                for k in range(2)
            ]
            deltas.append((pair, kind, jnp.concatenate(tiles, axis=1)))
    parts = [two_parts(delta) for _, _, delta in deltas]
    both = [jnp.concatenate(part, axis=0) for part in parts]
    for at in range(0, count, CHUNK):
        rows = slice(at, at + CHUNK)
        total = jnp.zeros((2 * outs, CHUNK), F32)
        small = jnp.zeros((outs, CHUNK), F32)
        for n, (pair, _, _) in enumerate(deltas):
            high_ref, low_ref = ((own_high, own_low), (other_high, other_low))[n % 2]
            total += dot(both[n], high_ref[step * pairs + pair, rows, :], TRANSPOSED)
            small += dot(parts[n][0], low_ref[step * pairs + pair, rows, :], TRANSPOSED)
        new_fitted_ref[:, rows] = fitted_ref[:, rows] - (
            total[:outs] + (total[outs:] + small)
        )

    new_weights_ref[...] = weights_ref[...]

    @pl.when(owners[step] == my_rank())
    def _():
        for pair, kind, delta in deltas:
            numbers = [index_tile(index_ref, step, 2 * pair + k, kind) for k in range(2)]
            pick = one_hot(count, jnp.concatenate(numbers, axis=1))
            new_weights_ref[...] -= exact_dot(delta, pick, TRANSPOSED)


def update(foreign, owners, delta, index, weights, fitted, own, other):
    shape = (weights.shape, F32)
    return call(
        functools.partial(update_kernel, foreign),
        "update",
        [shape, shape],
        owners,
        delta,
        index,
        weights,
        fitted,
        *own,
        *other,
        cost=pl.CostEstimate(
            flops=6 * own[0].size * weights.shape[0],
            bytes_accessed=4 * own[0].size,
            transcendentals=0,
        ),
    )


def local(points, weights, targets, fitted, preconditioner, owners, block_index):
    steps = block_index.shape[0]
    features = points.shape[1]
    groups = GRID[0] * GRID[1]
    lines = lax.axis_size("x")

    given = lax.all_gather(preconditioner, DP, axis=0)

    keep, send = pick_blocks(points.T, block_index)
    parcels = choose(owners, keep, exchange(send)).reshape(groups, -1, LANES)
    blocks = all_to_all(take(owners, all_to_all(parcels, ZY)), ZY)
    blocks = blocks.reshape(steps, FEATURE_ROWS, LANES)[:, :KEPT_ROWS]
    blocks = blocks.reshape(1, steps * KEPT_ROWS, LANES)
    own = all_to_all(jnp.broadcast_to(blocks, (lines, *blocks.shape[1:])), "x")
    other = exchange(own)

    data = (weights, targets, block_index)
    grad_own, *kern_own, rows, norms, parts = kernel_and_gradient(
        features, owners, (points.T,), *data, own, True
    )
    grad_theirs = exchange(grad_own)
    grad_other, *kern_other = kernel_and_gradient(
        features, owners, (rows, norms, parts), *data, other, False
    )
    grad = all_to_all(grad_other + grad_theirs, ZY)
    grad, given, own, other = lax.optimization_barrier((grad, given, own, other))
    grad = total(owners, grad)
    theirs = exchange(grad)
    between, given = between_blocks(features, owners, block_index, own, other, given)
    mine = run_chain(owners, grad, theirs, given, between)

    mine = all_to_all(jnp.broadcast_to(mine, (groups, *mine.shape)), ZY)
    theirs = exchange(mine)
    rest = (kern_own, kern_other)
    weights, fitted = update(0, owners, mine, block_index, weights, fitted, *rest)
    weights, fitted = update(1, owners, theirs, block_index, weights, fitted, *rest)
    return (weights, fitted)


def solution(mesh):
    grid = Mesh(mesh.devices.reshape(*GRID, mesh.shape["out"]), (*DP, "x"))
    return jax.shard_map(
        local,
        mesh=grid,
        in_specs=(
            P(DP, None),
            P("x", DP),
            P("x", DP),
            P("x", DP),
            P(None, DP, None),
            P(),
            P(),
        ),
        out_specs=(P("x", DP), P("x", DP)),
        check_vma=False,
    )
```

```python
import functools

import jax
import jax.numpy as jnp
from jax import lax
from jax.experimental import pallas as pl
from jax.experimental.pallas import tpu as pltpu
from jax.sharding import Mesh, PartitionSpec as P

LAMBDA = 0.5
GRID = (8, 8, 2)
ZY = ("z", "y")
DP = ("z", "y", "c")
FEATURE_ROWS = 512
KEPT_ROWS = 448
LANES = 128
CHUNK = 256
UNIT = 768
SHARE = 32
VMEM_BYTES = 16 * 1024 * 1024
BETWEEN_BYTES = 36 * 1024 * 1024
BF16 = jnp.bfloat16
F32 = jnp.float32
TRANSPOSED = (((1,), (1,)), ((), ()))
FIRST_DIMS = (((0,), (0,)), ((), ()))
WHOLE = pl.BlockSpec(memory_space=pltpu.VMEM)
FAR = pl.BlockSpec(memory_space=pltpu.HBM)


def call(
    kernel,
    name,
    shapes,
    owners,
    *args,
    in_specs=None,
    scratch=(),
    cost=None,
    vmem=VMEM_BYTES,
):
    return pl.pallas_call(
        kernel,
        grid_spec=pltpu.PrefetchScalarGridSpec(
            num_scalar_prefetch=1,
            grid=(),
            in_specs=in_specs or [WHOLE] * len(args),
            out_specs=[WHOLE] * len(shapes),
            scratch_shapes=list(scratch),
        ),
        out_shape=[jax.ShapeDtypeStruct(*shape) for shape in shapes],
        compiler_params=pltpu.CompilerParams(vmem_limit_bytes=vmem),
        cost_estimate=cost,
        name=name,
    )(owners, *args)


def my_rank():
    return (lax.axis_index("z") * GRID[1] + lax.axis_index("y")) * GRID[2] + lax.axis_index("c")


def exchange(value):
    return lax.ppermute(value, "c", [(0, 1), (1, 0)])


def all_to_all(value, axes):
    return lax.all_to_all(value, axes, 0, 0, tiled=True)


def two_parts(value):
    high = value.astype(BF16)
    return high, (value - high.astype(F32)).astype(BF16)


def three_parts(value):
    high = value.astype(BF16)
    rest = value - high.astype(F32)
    middle = rest.astype(BF16)
    return high, middle, (rest - middle.astype(F32)).astype(BF16)


def dot(left, right, dims=(((1,), (0,)), ((), ()))):
    return lax.dot_general(left, right, dims, preferred_element_type=F32)


def exact_dot(value, pick, dims=(((1,), (0,)), ((), ()))):
    rows = value.shape[0]
    terms = dot(jnp.concatenate(three_parts(value), axis=0), pick, dims)
    return terms[:rows] + (terms[rows : 2 * rows] + terms[2 * rows :])


def one_hot(count, numbers):
    rows = lax.broadcasted_iota(jnp.int32, (count, numbers.shape[1]), 0)
    return jnp.where(rows == numbers, 1.0, 0.0).astype(BF16)


def index_tile(index_ref, step, line, kind):
    at = pl.multiple_of((2 * line + kind) * LANES, LANES)
    tiles = index_ref[:, pl.ds(at, LANES)]
    return jnp.where(step == 0, tiles[0:1], tiles[1:2])


def pick_kernel(points_ref, index_ref, keep_ref, send_ref):
    features, count = points_ref.shape
    steps = index_ref.shape[0]
    core, line = lax.axis_index("c"), lax.axis_index("x")
    numbers = [
        index_tile(index_ref, step, line, kind)
        for kind in (core, 1 - core)
        for step in range(steps)
    ]
    picked = dot(points_ref[...], one_hot(count, jnp.concatenate(numbers, axis=1)))
    empty = jnp.zeros((FEATURE_ROWS - features, picked.shape[1]), F32)
    picked = jnp.concatenate([picked, empty], axis=0).astype(BF16)
    for place, ref in enumerate((keep_ref, send_ref)):
        for step in range(steps):
            at = (place * steps + step) * LANES
            ref[step] = picked[:, at : at + LANES]


def pick_blocks(points, index):
    shape = jax.ShapeDtypeStruct((index.shape[0], FEATURE_ROWS, LANES), BF16)
    block = pl.BlockSpec(shape.shape, lambda i: (0, 0, 0))
    return pl.pallas_call(
        pick_kernel,
        grid=(1,),
        in_specs=[pl.BlockSpec(array.shape, lambda i: (0, 0)) for array in (points, index)],
        out_specs=[block, block],
        out_shape=[shape, shape],
        compiler_params=pltpu.CompilerParams(vmem_limit_bytes=VMEM_BYTES),
        name="pick_blocks",
    )(points, index)


def choose_kernel(owners, keep_ref, got_ref, out_ref):
    core = lax.axis_index("c")
    for step in range(out_ref.shape[0]):
        mine = (owners[step] & 1) == core
        out_ref[step] = jnp.where(mine, keep_ref[step], got_ref[step])


def choose(owners, keep, got):
    return call(choose_kernel, "choose", [(keep.shape, BF16)], owners, keep, got)[0]


def take_kernel(owners, parcels_ref, out_ref):
    groups = parcels_ref.shape[0]
    per_step = groups // owners.shape[0]
    zy = lax.axis_index("z") * GRID[1] + lax.axis_index("y")
    holder = jnp.where(zy < per_step, owners[0], owners[1]) >> 1
    piece = parcels_ref[pl.ds(holder, 1)]
    out_ref[...] = jnp.broadcast_to(piece, out_ref.shape)


def take(owners, parcels):
    return call(take_kernel, "take", [(parcels.shape, BF16)], owners, parcels)[0]


def prepare(features, points_ref, weights_ref, rows_ref, norms_ref, parts_ref):
    count = points_ref.shape[1]
    outs = weights_ref.shape[0]
    gamma = 2.0 / features
    empty = jnp.zeros((KEPT_ROWS - features, LANES), F32)
    for at in range(0, count, LANES):
        rows = slice(at, at + LANES)
        wide = jnp.concatenate([points_ref[:, rows].astype(F32), empty], axis=0)
        wide = jnp.transpose(wide)
        rows_ref[rows, :] = wide.astype(BF16)
        norms_ref[rows, :] = gamma * jnp.sum(wide * wide, axis=1, keepdims=True)
    high, low = two_parts(weights_ref[...])
    parts_ref[:outs, :] = high
    parts_ref[outs:, :] = low


def kernel_body(
    features,
    foreign,
    owners,
    rows_ref,
    norms_ref,
    parts_ref,
    weights_ref,
    targets_ref,
    index_ref,
    blocks_ref,
    grad_ref,
    high_ref,
    low_ref,
):
    count = rows_ref.shape[0]
    outs = weights_ref.shape[0]
    pairs = blocks_ref.shape[0] // 2
    steps = index_ref.shape[0]
    gamma = 2.0 / features

    blocks, block_norms, grads = [], [], []
    for step in range(steps):
        rows = slice(step * KEPT_ROWS, (step + 1) * KEPT_ROWS)
        for pair in range(pairs):
            block = jnp.concatenate(
                [blocks_ref[2 * pair, rows, :], blocks_ref[2 * pair + 1, rows, :]], axis=1
            )
            wide = block.astype(F32)
            blocks.append(block)
            block_norms.append(gamma * jnp.sum(wide * wide, axis=0, keepdims=True))
            grads.append(jnp.zeros((outs, 2 * LANES), F32))

    units = [(n, at) for n in range(steps * pairs) for at in range(0, count, UNIT)]

    def cross(n, at):
        return dot(rows_ref[at : at + UNIT, :], blocks[n])

    ahead = cross(*units[0])
    for place, (n, at) in enumerate(units):
        now = ahead
        if place + 1 < len(units):
            ahead = cross(*units[place + 1])
        rows = slice(at, at + UNIT)
        kern = jnp.exp((2.0 * gamma) * now - (norms_ref[rows, :] + block_norms[n]))
        high, low = two_parts(kern)
        high_ref[n, rows, :] = high
        low_ref[n, rows, :] = low
        both = dot(parts_ref[:, rows], high)
        grads[n] += both[:outs] + both[outs:] + dot(parts_ref[:outs, rows], low)

    for n, grad in enumerate(grads):
        for k in range(2):
            tile = 2 * n + k
            part = grad[:, k * LANES : (k + 1) * LANES]
            grad_ref[:, tile : tile + 1, :] = part.reshape(outs, 1, LANES)

    rank = my_rank()
    kind = lax.axis_index("c") ^ foreign
    for step in range(steps):

        @pl.when(owners[step] == rank)
        def _():
            own = LAMBDA * weights_ref[...] - targets_ref[...]
            for pair in range(pairs):
                numbers = [index_tile(index_ref, step, 2 * pair + k, kind) for k in range(2)]
                term = exact_dot(own, one_hot(count, jnp.concatenate(numbers, axis=1)))
                for k in range(2):
                    tile = (step * pairs + pair) * 2 + k
                    part = term[:, k * LANES : (k + 1) * LANES]
                    grad_ref[:, tile : tile + 1, :] += part.reshape(outs, 1, LANES)


def first_kernel(features, owners, points, weights, targets, index, blocks, *rest):
    grad, high, low, rows, norms, parts = rest
    prepare(features, points, weights, rows, norms, parts)
    kernel_body(
        features, 0, owners, rows, norms, parts, weights, targets, index, blocks,
        grad, high, low,
    )


def second_kernel(features, *refs):
    kernel_body(features, 1, *refs)


def kernel_and_gradient(features, owners, data, weights, targets, index, blocks, first):
    outs, count = weights.shape
    tiles = index.shape[0] * blocks.shape[0]
    kern = (tiles // 2, count, 2 * LANES)
    shapes = [((outs, tiles, LANES), F32), (kern, BF16), (kern, BF16)]
    if first:
        shapes += [((count, KEPT_ROWS), BF16), ((count, 1), F32), ((2 * outs, count), BF16)]
    return call(
        functools.partial(first_kernel if first else second_kernel, features),
        "first_half" if first else "second_half",
        shapes,
        owners,
        *data,
        weights,
        targets,
        index,
        blocks,
        cost=pl.CostEstimate(
            flops=tiles * LANES * count * (2 * KEPT_ROWS + 6 * outs),
            bytes_accessed=4 * tiles * LANES * count,
            transcendentals=tiles * LANES * count,
        ),
    )


def between_kernel(
    features, owners, index_ref, own_ref, other_ref, given_far, out_ref, given_ref, sems
):
    copies = [
        pltpu.make_async_copy(given_far.at[rows], given_ref.at[rows], sems.at[n])
        for n, rows in enumerate(slice(at, at + SHARE) for at in range(0, given_ref.shape[0], SHARE))
    ]
    for copy in copies:
        copy.start()
    lines = own_ref.shape[0]
    gamma = 2.0 / features
    core = lax.axis_index("c")

    def tile(step, line, kind):
        at = step * KEPT_ROWS
        rows = slice(at, at + KEPT_ROWS)
        return jnp.where(core == kind, own_ref[line, rows, :], other_ref[line, rows, :])

    places = [(line, kind) for line in range(lines) for kind in range(2)]
    second = jnp.concatenate([tile(1, *place) for place in places], axis=1)
    wide = second.astype(F32)
    second_norm = gamma * jnp.sum(wide * wide, axis=0, keepdims=True)
    second_index = index_ref[1:2, :]
    extra = jnp.where(owners[0] == owners[1], LAMBDA, 0.0)
    for n, place in enumerate(places):
        first = tile(0, *place)
        wide = first.astype(F32)
        square = jnp.sum(wide * wide, axis=0, keepdims=True)
        first_norm = gamma * jnp.transpose(jnp.broadcast_to(square, (LANES, LANES)))[:, :1]
        first_index = jnp.transpose(
            jnp.broadcast_to(
                index_ref[0:1, n * LANES : (n + 1) * LANES].astype(F32), (LANES, LANES)
            )
        )[:, :1].astype(jnp.int32)
        cross = dot(first, second, FIRST_DIMS)
        kern = jnp.exp((2.0 * gamma) * cross - (first_norm + second_norm))
        out_ref[n * LANES : (n + 1) * LANES, :] = kern + jnp.where(
            first_index == second_index, extra, 0.0
        )
    for copy in copies:
        copy.wait()


def between_blocks(features, owners, index, own, other, given):
    block = index.shape[1]
    return call(
        functools.partial(between_kernel, features),
        "between_blocks",
        [((block, block), F32), (given.shape, F32)],
        owners,
        index,
        own,
        other,
        given,
        in_specs=[WHOLE] * 3 + [FAR],
        scratch=[pltpu.SemaphoreType.DMA((given.shape[0] // SHARE,))],
        cost=pl.CostEstimate(
            flops=2 * block * block * KEPT_ROWS,
            bytes_accessed=4 * block * block,
            transcendentals=block * block,
        ),
        vmem=BETWEEN_BYTES,
    )


def chain_kernel(owners, mine_ref, theirs_ref, given_ref, between_ref, out_ref, grads):
    tiles = out_ref.shape[0]
    block = between_ref.shape[0]
    rows = given_ref.shape[2]
    lines = tiles // 2
    core = lax.axis_index("c")
    for step in range(2):
        for line in range(lines):
            at = slice(step * lines + line, step * lines + line + 1)
            for kind in range(2):
                lanes = slice((2 * line + kind) * LANES, (2 * line + kind + 1) * LANES)
                grads[step : step + 1, lanes] = jnp.where(
                    core == kind, theirs_ref[at, :], mine_ref[at, :]
                )

    diagonal = lax.broadcasted_iota(jnp.int32, (LANES, LANES), 0) == lax.broadcasted_iota(
        jnp.int32, (LANES, LANES), 1
    )
    share = LANES // rows
    correction = jnp.zeros((8, block), F32)
    for step in range(2):
        grad = grads[step : step + 1, :]
        if step == 1:
            grad = grad - jnp.sum(correction, axis=0, keepdims=True)
        for n in range(tiles):
            given = given_ref[n * share : (n + 1) * share, step].reshape(LANES, block)
            delta = jnp.sum(given * grad, axis=1, keepdims=True)
            row = jnp.sum(jnp.where(diagonal, delta, 0.0), axis=0, keepdims=True)
            if step == 0:
                out_ref[n : n + 1, :] = row
            else:
                out_ref[n : n + 1, :] = jnp.where(core == 0, out_ref[n : n + 1, :], row)
            if step == 0:
                product = delta * between_ref[n * LANES : (n + 1) * LANES, :]
                correction += jnp.sum(product.reshape(-1, 8, block), axis=0)


def run_chain(owners, mine, theirs, given, between):
    block = given.shape[3]
    return call(
        chain_kernel,
        "run_chain",
        [((block // LANES, LANES), F32)],
        owners,
        mine,
        theirs,
        given,
        between,
        scratch=[pltpu.VMEM((2, block), F32)],
    )[0]


def total_kernel(owners, parts_ref, out_ref):
    total = parts_ref[0]
    for n in range(1, parts_ref.shape[0]):
        total += parts_ref[n]
    out_ref[...] = total


def total(owners, parts):
    return call(total_kernel, "total", [(parts.shape[1:], F32)], owners, parts)[0]


def update_kernel(
    foreign,
    owners,
    delta_ref,
    index_ref,
    weights_ref,
    fitted_ref,
    own_high,
    own_low,
    other_high,
    other_low,
    new_weights_ref,
    new_fitted_ref,
):
    core = lax.axis_index("c")
    step = core ^ foreign
    outs, count = weights_ref.shape
    pairs = own_high.shape[0] // 2

    deltas = []
    for pair in range(pairs):
        for kind in (core, 1 - core):
            tiles = [
                delta_ref[:, pl.ds(2 * (2 * pair + k) + kind, 1), :].reshape(outs, LANES)
                for k in range(2)
            ]
            deltas.append((pair, kind, jnp.concatenate(tiles, axis=1)))
    parts = [two_parts(delta) for _, _, delta in deltas]
    both = [jnp.concatenate(part, axis=0) for part in parts]
    for at in range(0, count, CHUNK):
        rows = slice(at, at + CHUNK)
        total = jnp.zeros((2 * outs, CHUNK), F32)
        small = jnp.zeros((outs, CHUNK), F32)
        for n, (pair, _, _) in enumerate(deltas):
            high_ref, low_ref = ((own_high, own_low), (other_high, other_low))[n % 2]
            total += dot(both[n], high_ref[step * pairs + pair, rows, :], TRANSPOSED)
            small += dot(parts[n][0], low_ref[step * pairs + pair, rows, :], TRANSPOSED)
        new_fitted_ref[:, rows] = fitted_ref[:, rows] - (
            total[:outs] + (total[outs:] + small)
        )

    new_weights_ref[...] = weights_ref[...]

    @pl.when(owners[step] == my_rank())
    def _():
        for pair, kind, delta in deltas:
            numbers = [index_tile(index_ref, step, 2 * pair + k, kind) for k in range(2)]
            pick = one_hot(count, jnp.concatenate(numbers, axis=1))
            new_weights_ref[...] -= exact_dot(delta, pick, TRANSPOSED)


def update(foreign, owners, delta, index, weights, fitted, own, other):
    shape = (weights.shape, F32)
    return call(
        functools.partial(update_kernel, foreign),
        "update",
        [shape, shape],
        owners,
        delta,
        index,
        weights,
        fitted,
        *own,
        *other,
        cost=pl.CostEstimate(
            flops=6 * own[0].size * weights.shape[0],
            bytes_accessed=4 * own[0].size,
            transcendentals=0,
        ),
    )


def local(points, weights, targets, fitted, preconditioner, owners, block_index):
    steps = block_index.shape[0]
    features = points.shape[1]
    groups = GRID[0] * GRID[1]
    lines = lax.axis_size("x")

    given = lax.all_gather(preconditioner, DP, axis=0)

    keep, send = pick_blocks(points.T, block_index)
    parcels = choose(owners, keep, exchange(send)).reshape(groups, -1, LANES)
    blocks = all_to_all(take(owners, all_to_all(parcels, ZY)), ZY)
    blocks = blocks.reshape(steps, FEATURE_ROWS, LANES)[:, :KEPT_ROWS]
    blocks = blocks.reshape(1, steps * KEPT_ROWS, LANES)
    own = all_to_all(jnp.broadcast_to(blocks, (lines, *blocks.shape[1:])), "x")
    other = exchange(own)

    data = (weights, targets, block_index)
    grad_own, *kern_own, rows, norms, parts = kernel_and_gradient(
        features, owners, (points.T,), *data, own, True
    )
    grad_theirs = exchange(grad_own)
    grad_other, *kern_other = kernel_and_gradient(
        features, owners, (rows, norms, parts), *data, other, False
    )
    grad = all_to_all(grad_other + grad_theirs, ZY)
    grad, given, own, other = lax.optimization_barrier((grad, given, own, other))
    grad = total(owners, grad)
    theirs = exchange(grad)
    between, given = between_blocks(features, owners, block_index, own, other, given)
    mine = run_chain(owners, grad, theirs, given, between)

    mine = all_to_all(jnp.broadcast_to(mine, (groups, *mine.shape)), ZY)
    theirs = exchange(mine)
    rest = (kern_own, kern_other)
    weights, fitted = update(0, owners, mine, block_index, weights, fitted, *rest)
    weights, fitted = update(1, owners, theirs, block_index, weights, fitted, *rest)
    return (weights, fitted)


def solution(mesh):
    grid = Mesh(mesh.devices.reshape(*GRID, mesh.shape["out"]), (*DP, "x"))
    return jax.shard_map(
        local,
        mesh=grid,
        in_specs=(
            P(DP, None),
            P("x", DP),
            P("x", DP),
            P("x", DP),
            P(None, DP, None),
            P(),
            P(),
        ),
        out_specs=(P("x", DP), P("x", DP)),
        check_vma=False,
    )
```
